32 devices in a mesh: req: 8 (over z, y), tp: 4 (over x, core).
Axes of the slice: x: 2, y: 2, z: 4, core: 2. Of those that a mesh axis runs over, the one named last changes fastest.
Arguments:
- tokens: bfloat16 [8192, 1792], P(('req', 'tp')), may hold values from -6 to 6
- norm_gain: float32 [1792], replicated, may hold values from 0.25 to 1.75
- ffn_gain: float32 [1792], replicated, may hold values from 0.25 to 1.75
- mix_weight: bfloat16 [1792, 4, 1792], P('req', None, 'tp'), may hold values from -0.125 to 0.125
- out_weight: bfloat16 [1792, 1792], P('tp', 'req'), may hold values from -0.125 to 0.125
- ffn_weight: bfloat16 [1792, 2, 7168], P('req', None, 'tp'), may hold values from -0.125 to 0.125
- down_weight: bfloat16 [7168, 1792], P('tp', 'req'), may hold values from -0.0625 to 0.0625
- conv_taps: float32 [3, 1792], P(None, 'tp'), may hold values from -3 to 3
- past_cache: bfloat16 [8, 2, 64, 1792], P('req', None, None, 'tp'), may hold values from -210 to 210
- cached_len: int32 [8], P('req'), may hold values from 0 to 8192, as said below
Outputs:
- layer_out: bfloat16 [8192, 1792], P(('req', 'tp'))
- new_cache: bfloat16 [8, 2, 64, 1792], P('req', None, None, 'tp')
The draws below stay inside these ranges and needn't reach their ends.
Inputs may be any that keep to these rules, and one draw needn't show every extreme that they name: `cached_len`: one request has exactly 8192 cached positions and another fewer than 64.
All inputs are finite; a program needn't handle non-finite values.
Results may differ from the reference program's by a relative error of at most 0.02.
Values may be sent and summed in bfloat16 or wider, within the bound.
A program may use at most 128 MiB of HBM per device.

```python
import math
import jax
import jax.numpy as jnp
from jax import lax

D = 1792
HD = 112
FF_WIN = 7168
WIN = 64
KCONV = 3
MAXLEN = 8192
SPAN = 1024
REQS = 8
TOKENS = 8192
N_TP = 4


def draw_cached_len(key, part):
    keys_list = jax.random.split(key, 5)
    left_draw = jax.random.randint(keys_list[0], (REQS,), 0, MAXLEN + 1)
    right_draw = jax.random.randint(keys_list[1], (REQS,), 0, MAXLEN + 1)
    lengths = left_draw * right_draw // MAXLEN
    top_slot = jax.random.randint(keys_list[2], (), 0, REQS)
    low_slot = (top_slot + 1 + jax.random.randint(keys_list[3], (), 0, REQS - 1)) % REQS
    low_value = jax.random.randint(keys_list[4], (), 0, WIN)
    request_ids = jnp.arange(REQS)
    lengths = jnp.where(request_ids == top_slot, MAXLEN, lengths)
    lengths = jnp.where(request_ids == low_slot, low_value, lengths)
    return lengths.astype(jnp.int32)


def draw_past_cache(key, part):
    keys_list = jax.random.split(jax.random.fold_in(key, 11), 1)
    values = jax.random.normal(keys_list[0], (REQS, 2, WIN, D), jnp.float32)
    return values.astype(jnp.bfloat16)


def block_scale(stream_key, shape, pieces, low, high):
    loudness, own = 1.0, jax.random.fold_in(stream_key, 6)
    for position, blocks in pieces:
        steps = jnp.exp(jax.random.uniform(jax.random.fold_in(own, position), (blocks,), jnp.float32, low / len(pieces), high / len(pieces)))
        loudness = loudness * jnp.repeat(steps, shape[position] // blocks).reshape([-1 if axis == position else 1 for axis in range(len(shape))])
    return loudness


def centred(stream_key, shape, scale, reach, pieces=(), kind=jnp.bfloat16):
    array = jax.random.normal(stream_key, shape, jnp.float32) * scale
    if len(pieces) > 0:
        array = block_scale(stream_key, shape, pieces, -0.22, 0.18) * array
    return jnp.clip(array, min=-reach, max=reach).astype(kind)


def setup_inputs(seed: int = 0) -> dict:
    seeds = jax.random.split(jax.random.key(seed), 11)
    return {
        "tokens": centred(seeds[0], (TOKENS, D), 1.0, 6.0, ((0, 32),)),
        "norm_gain": jnp.clip(1.0 + 0.15 * jax.random.normal(seeds[1], (D,), jnp.float32), 0.25, 1.75),
        "ffn_gain": jnp.clip(1.0 + 0.15 * jax.random.normal(seeds[2], (D,), jnp.float32), 0.25, 1.75),
        "mix_weight": centred(seeds[3], (D, 4, D), D ** -0.5, 0.125, ((0, 8), (2, 4))),
        "out_weight": centred(seeds[4], (D, D), D ** -0.5, 0.125, ((0, 4), (1, 8))),
        "ffn_weight": centred(seeds[5], (D, 2, FF_WIN), D ** -0.5, 0.125, ((0, 8), (2, 4))),
        "down_weight": centred(seeds[6], (FF_WIN, D), FF_WIN ** -0.5, 0.0625, ((0, 4), (1, 8))),
        "conv_taps": centred(seeds[7], (KCONV, D), 0.6, 3.0, ((1, 4),), jnp.float32),
        "past_cache": draw_past_cache(jax.random.fold_in(seeds[10], 71), 0),
        "cached_len": draw_cached_len(jax.random.fold_in(seeds[10], 71), 0),
    }


def normed(row_vals, gain):
    floats = row_vals.astype(jnp.float32)
    scaled = floats * lax.rsqrt(lax.optimization_barrier(jnp.mean(floats * floats, axis=-1, keepdims=True)) + 1e-05)
    return (scaled * gain.astype(jnp.float32)).astype(jnp.bfloat16)

def window_attend(queries, key_rows, value_rows, length, window):
    row_count, head_count, head_size = queries.shape
    block_rows = min(512, row_count)
    score_scale = 1.0 / math.sqrt(head_size)

    def one_block(block_index):
        begin_row = block_index * block_rows
        query_block = lax.dynamic_slice_in_dim(queries, begin_row, block_rows, 0)
        key_block = lax.dynamic_slice_in_dim(key_rows, begin_row, block_rows + window, 0)
        value_block = lax.dynamic_slice_in_dim(value_rows, begin_row, block_rows + window, 0)
        scores = jnp.einsum('qhd,khd->hqk', query_block.astype(jnp.float32), key_block.astype(jnp.float32)) * score_scale
        row_ids = begin_row + jnp.arange(block_rows, dtype=jnp.int32)[:, None]
        col_ids = begin_row + jnp.arange(block_rows + window, dtype=jnp.int32)[None, :]
        usable = (col_ids > row_ids) & (col_ids <= row_ids + window) & (col_ids >= window - length)
        scores = jnp.where(usable[None], scores, -1e+30)
        row_max = lax.optimization_barrier(jnp.max(scores, axis=-1, keepdims=True))
        exponent = jnp.exp(scores - row_max)
        weights = (exponent / lax.optimization_barrier(jnp.sum(exponent, axis=-1, keepdims=True))).astype(jnp.bfloat16)
        return jnp.einsum('hqk,khd->qhd', weights.astype(jnp.float32), value_block.astype(jnp.float32))
    blocks = lax.map(one_block, jnp.arange(row_count // block_rows, dtype=jnp.int32))
    return blocks.reshape(row_count, head_count, head_size)

def mix_request(projected, cache_rows, length, tap_table, window, head_size):
    row_count, feat_width = (projected.shape[0], projected.shape[2])
    time_order = (length + jnp.arange(window, dtype=jnp.int32)) % window
    earlier = cache_rows[:, time_order]
    key_rows = jnp.concatenate([earlier[0], projected[:, 1]], axis=0)
    value_rows = jnp.concatenate([earlier[1], projected[:, 2]], axis=0)
    head_count = feat_width // head_size
    attended = window_attend(projected[:, 0].reshape(row_count, head_count, head_size), key_rows.reshape(-1, head_count, head_size), value_rows.reshape(-1, head_count, head_size), length, window).reshape(row_count, feat_width)
    positions = jnp.arange(window + row_count, dtype=jnp.int32)
    alive_mask = (positions >= window - length)[:, None]
    masked_values = jnp.where(alive_mask, value_rows.astype(jnp.float32), jnp.float32(0.0))
    tap_count = tap_table.shape[0]
    convolved = jnp.zeros((row_count, feat_width), jnp.float32)
    for tap_index in range(tap_count):
        begin_row = window - (tap_count - 1) + tap_index
        convolved = convolved + tap_table[tap_index].astype(jnp.float32) * masked_values[begin_row:begin_row + row_count]
    mixed_heads = (attended + projected[:, 3].astype(jnp.float32) * convolved).astype(jnp.bfloat16)
    slot_source = row_count - window + (jnp.arange(window, dtype=jnp.int32) - length - row_count) % window
    renewed = jnp.stack([projected[:, 1], projected[:, 2]])[:, slot_source]
    return (mixed_heads, renewed)

def reference(tokens, norm_gain, ffn_gain, mix_weight, out_weight, ffn_weight, down_weight, conv_taps, past_cache, cached_len):
    feat_group = D // N_TP
    ffn_group = FF_WIN // N_TP

    def one_request(items):
        token_rows, cache_rows, length = items
        normed_in = normed(token_rows, norm_gain)
        projected = jnp.dot(normed_in, mix_weight.reshape(D, 4 * D), preferred_element_type=jnp.float32)
        projected = projected.astype(jnp.bfloat16).reshape(SPAN, 4, D)
        mixed_heads, renewed = mix_request(projected, cache_rows, length, conv_taps, WIN, HD)
        attn_sum = jnp.zeros((SPAN, D), jnp.float32)
        for group_id in range(N_TP):
            group_begin = group_id * feat_group
            term_rows = jnp.dot(mixed_heads[:, group_begin:group_begin + feat_group], out_weight[group_begin:group_begin + feat_group], preferred_element_type=jnp.float32).astype(jnp.bfloat16)
            attn_sum = attn_sum + lax.optimization_barrier(term_rows).astype(jnp.float32)
        residual = (token_rows.astype(jnp.float32) + attn_sum).astype(jnp.bfloat16)
        ffn_in = normed(residual, ffn_gain)
        gate_up = jnp.dot(ffn_in, ffn_weight.reshape(D, 2 * FF_WIN), preferred_element_type=jnp.float32)
        activated = (jax.nn.silu(gate_up[:, :FF_WIN]) * gate_up[:, FF_WIN:]).astype(jnp.bfloat16)
        ffn_sum = jnp.zeros((SPAN, D), jnp.float32)
        for group_id in range(N_TP):
            group_begin = group_id * ffn_group
            term_rows = jnp.dot(activated[:, group_begin:group_begin + ffn_group], down_weight[group_begin:group_begin + ffn_group], preferred_element_type=jnp.float32).astype(jnp.bfloat16)
            ffn_sum = ffn_sum + lax.optimization_barrier(term_rows).astype(jnp.float32)
        layer_out = (residual.astype(jnp.float32) + ffn_sum).astype(jnp.bfloat16)
        return (layer_out, renewed)
    layer_out, new_cache = lax.map(one_request, (tokens.reshape(REQS, SPAN, D), past_cache, cached_len))
    return (layer_out.reshape(TOKENS, D), new_cache)
```

```python
import functools
import math

import jax
import jax.numpy as jnp
import numpy as np
from jax import lax
from jax.experimental import pallas as pl
from jax.experimental.pallas import tpu as pltpu
from jax.sharding import PartitionSpec as P

HD = 112
WIN = 64


def normed(row_vals, gain):
    floats = row_vals.astype(jnp.float32)
    scaled = floats * lax.rsqrt(jnp.mean(floats * floats, axis=-1, keepdims=True) + 1e-05)
    return (scaled * gain).astype(jnp.bfloat16)


def window_attend(queries, key_rows, value_rows, length, window):
    row_count, head_count, head_size = queries.shape
    block_rows = min(512, row_count)
    score_scale = 1.0 / math.sqrt(head_size)

    def one_block(block_index):
        begin_row = block_index * block_rows
        query_block = lax.dynamic_slice_in_dim(queries, begin_row, block_rows, 0)
        key_block = lax.dynamic_slice_in_dim(key_rows, begin_row, block_rows + window, 0)
        value_block = lax.dynamic_slice_in_dim(value_rows, begin_row, block_rows + window, 0)
        scores = (
            jnp.einsum("qhd,khd->hqk", query_block, key_block, preferred_element_type=jnp.float32)
            * score_scale
        )
        row_ids = begin_row + jnp.arange(block_rows, dtype=jnp.int32)[:, None]
        col_ids = begin_row + jnp.arange(block_rows + window, dtype=jnp.int32)[None, :]
        usable = (col_ids > row_ids) & (col_ids <= row_ids + window) & (col_ids >= window - length)
        scores = jnp.where(usable[None], scores, -1e30)
        row_max = jnp.max(scores, axis=-1, keepdims=True)
        exponent = jnp.exp(scores - row_max)
        weights = (exponent / jnp.sum(exponent, axis=-1, keepdims=True)).astype(jnp.bfloat16)
        return jnp.einsum("hqk,khd->qhd", weights, value_block, preferred_element_type=jnp.float32)

    blocks = lax.map(one_block, jnp.arange(row_count // block_rows, dtype=jnp.int32))
    return blocks.reshape(row_count, head_count, head_size)


def mix_request(projected, cache_rows, length, tap_table, window, head_size):
    row_count, feat_width = (projected.shape[0], projected.shape[2])
    time_order = (length + jnp.arange(window, dtype=jnp.int32)) % window
    earlier = cache_rows[:, time_order]
    key_rows = jnp.concatenate([earlier[0], projected[:, 1]], axis=0)
    value_rows = jnp.concatenate([earlier[1], projected[:, 2]], axis=0)
    head_count = feat_width // head_size
    attended = window_attend(
        projected[:, 0].reshape(row_count, head_count, head_size),
        key_rows.reshape(-1, head_count, head_size),
        value_rows.reshape(-1, head_count, head_size),
        length,
        window,
    ).reshape(row_count, feat_width)
    positions = jnp.arange(window + row_count, dtype=jnp.int32)
    alive_mask = (positions >= window - length)[:, None]
    masked_values = jnp.where(alive_mask, value_rows.astype(jnp.float32), jnp.float32(0.0))
    tap_count = tap_table.shape[0]
    convolved = jnp.zeros((row_count, feat_width), jnp.float32)
    for tap_index in range(tap_count):
        begin_row = window - (tap_count - 1) + tap_index
        convolved = (
            convolved + tap_table[tap_index] * masked_values[begin_row : begin_row + row_count]
        )
    mixed_heads = (attended + projected[:, 3].astype(jnp.float32) * convolved).astype(jnp.bfloat16)
    slot_source = (
        row_count - window + (jnp.arange(window, dtype=jnp.int32) - length - row_count) % window
    )
    renewed = jnp.stack([projected[:, 1], projected[:, 2]])[:, slot_source]
    return (mixed_heads, renewed)


def add_rows(left, shard_piece):
    return jnp.dot(
        left, shard_piece.reshape(shard_piece.shape[0], -1), preferred_element_type=jnp.float32
    )


def local(
    tokens,
    norm_gain,
    ffn_gain,
    mix_weight,
    out_weight,
    ffn_weight,
    down_weight,
    conv_taps,
    past_cache,
    cached_len,
):
    feat_width = mix_weight.shape[2]
    ffn_width = ffn_weight.shape[2]
    normed_all = lax.all_gather(normed(tokens, norm_gain), "tp", axis=0, tiled=True)
    row_total = normed_all.shape[0]
    projected = add_rows(normed_all, lax.all_gather(mix_weight, "req", axis=0, tiled=True))
    projected = projected.astype(jnp.bfloat16).reshape(row_total, 4, feat_width)
    mixed_heads, renewed = mix_request(projected, past_cache[0], cached_len[0], conv_taps, WIN, HD)
    out_columns = lax.all_gather(out_weight, "req", axis=1, tiled=True)
    attn_part = lax.psum_scatter(
        jnp.dot(mixed_heads, out_columns, preferred_element_type=jnp.float32).astype(jnp.bfloat16),
        "tp",
        scatter_dimension=0,
        tiled=True,
    ).astype(jnp.float32)
    residual = (tokens.astype(jnp.float32) + attn_part).astype(jnp.bfloat16)
    ffn_in = lax.all_gather(normed(residual, ffn_gain), "tp", axis=0, tiled=True)
    gate_up = add_rows(ffn_in, lax.all_gather(ffn_weight, "req", axis=0, tiled=True))
    down_columns = lax.all_gather(down_weight, "req", axis=1, tiled=True)
    activated = (jax.nn.silu(gate_up[:, :ffn_width]) * gate_up[:, ffn_width:]).astype(jnp.bfloat16)
    ffn_part = lax.psum_scatter(
        jnp.dot(activated, down_columns, preferred_element_type=jnp.float32).astype(jnp.bfloat16),
        "tp",
        scatter_dimension=0,
        tiled=True,
    ).astype(jnp.float32)
    layer_out = (residual.astype(jnp.float32) + ffn_part).astype(jnp.bfloat16)
    return (layer_out, renewed[None])

MESH = pl.DeviceIdType.MESH


def ring_spot(req_index, ring_size):
    z_index, y_index = req_index // 2, req_index % 2
    return z_index * (1 - y_index) + (ring_size - 1 - z_index) * y_index


def spot_req(spot, ring_size):
    side = spot // (ring_size // 2)
    return 2 * (spot * (1 - side) + (ring_size - 1 - spot) * side) + side


def layer_kernel(
    ring_size,
    group_size,
    window,
    head_count,
    head_size,
    tokens_ref,
    norm_gain_ref,
    ffn_gain_ref,
    taps_ref,
    cache_ref,
    length_ref,
    spread_ref,
    mix_ref,
    out_ref,
    ffn_ref,
    down_ref,
    ffn_sum_ref,
    residual_ref,
    renewed_ref,
    mix_all,
    out_all,
    ffn_all,
    down_all,
    normed_all,
    ffn_in_all,
    key_rows,
    value_rows,
    mixed,
    attn_got,
    shared,
    down_part,
    down_got,
    ring_send,
    ring_recv,
    own_sem,
    gather_send,
    gather_recv,
    attn_send,
    attn_recv,
    ffn_send,
    ffn_recv,
    down_send,
    down_recv,
):
    my_req, my_tp = lax.axis_index("req"), lax.axis_index("tp")
    spot = ring_spot(my_req, ring_size)
    right = spot_req((spot + 1) % ring_size, ring_size)
    left = spot_req((spot + ring_size - 1) % ring_size, ring_size)
    own_rows, width = tokens_ref.shape
    row_total = own_rows * group_size
    shard_rows = mix_ref.shape[0]
    half = shard_rows // 2
    feat_width = out_all.shape[1]
    hidden = ffn_all.shape[1] // 2
    half_cols = mix_ref.shape[1] // 2
    wide = head_count * 128
    last = ring_size - 2

    streams = [
        (out_ref, out_all, 0, feat_width),
        (mix_ref, mix_all, 0, half_cols),
        (mix_ref, mix_all, half_cols, half_cols),
        (ffn_ref, ffn_all, 0, hidden),
        (ffn_ref, ffn_all, hidden, hidden),
        (down_ref, down_all, 0, hidden // 2),
        (down_ref, down_all, hidden // 2, hidden // 2),
    ]
    mix_phase, ffn_phase, down_phase = (0, 1, 2), (3, 4), (5, 6)

    def shard_req(direction, step):
        if direction == 0:
            return spot_req((spot + ring_size - step) % ring_size, ring_size)
        return spot_req((spot + step) % ring_size, ring_size)

    def half_begin(direction, step):
        return pl.multiple_of(shard_req(direction, step) * shard_rows + direction * half, 16)

    def ring_copy(stream, direction, step, first):
        source, whole, col_begin, col_count = streams[stream]
        cols = pl.ds(col_begin, col_count)
        place = whole.at[pl.ds(half_begin(direction, step), half), cols]
        sem_index = (stream * 2 + direction) * (ring_size - 1) + step
        return pltpu.make_async_remote_copy(
            src_ref=source.at[pl.ds(direction * half, half), cols] if first else place,
            dst_ref=place,
            send_sem=ring_send.at[sem_index],
            recv_sem=ring_recv.at[sem_index],
            device_id={"req": left if direction else right},
            device_id_type=MESH,
        )

    def ring_arrived(stream, direction, step):
        _, whole, col_begin, col_count = streams[stream]
        place = whole.at[
            pl.ds(half_begin(direction, step + 1), half), pl.ds(col_begin, col_count)
        ]
        sem_index = (stream * 2 + direction) * (ring_size - 1) + step
        pltpu.make_async_remote_copy(
            src_ref=place,
            dst_ref=place,
            send_sem=ring_send.at[sem_index],
            recv_sem=ring_recv.at[sem_index],
            device_id={"req": left if direction else right},
            device_id_type=MESH,
        ).wait_recv()

    def begin(phase):
        for stream in phase:
            for direction in range(2):
                ring_copy(stream, direction, 0, True).start()

    def tick(phase, step):
        for stream in phase:
            for direction in range(2):
                ring_arrived(stream, direction, step - 1)
                ring_copy(stream, direction, step, False).start()

    def ticks(phase, low, high):
        @pl.loop(low, high)
        def _(step):
            tick(phase, step)

    def finish(phase):
        for stream in phase:
            for direction in range(2):
                ring_arrived(stream, direction, last)

    def own_copy(index):
        source, whole = ((mix_ref, mix_all), (out_ref, out_all), (ffn_ref, ffn_all), (down_ref, down_all))[index]
        begin_row = pl.multiple_of(my_req * shard_rows, 16)
        return pltpu.make_async_copy(
            source, whole.at[pl.ds(begin_row, shard_rows)], own_sem.at[index]
        )

    def peer(distance):
        return (my_tp + distance) % group_size

    def group_rows(member):
        return pl.ds(pl.multiple_of(member * own_rows, 16), own_rows)

    def gather_copy(whole, sends, recvs, distance):
        rows = whole.at[group_rows(my_tp)]
        return pltpu.make_async_remote_copy(
            src_ref=rows,
            dst_ref=rows,
            send_sem=sends.at[distance - 1],
            recv_sem=recvs.at[distance - 1],
            device_id={"tp": peer(distance)},
            device_id_type=MESH,
        )

    def gather_arrived(whole, sends, recvs, distance):
        rows = whole.at[group_rows((my_tp + group_size - distance) % group_size)]
        pltpu.make_async_remote_copy(
            src_ref=rows,
            dst_ref=rows,
            send_sem=sends.at[distance - 1],
            recv_sem=recvs.at[distance - 1],
            device_id={"tp": peer(distance)},
            device_id_type=MESH,
        ).wait_recv()

    def attn_copy(distance):
        return pltpu.make_async_remote_copy(
            src_ref=normed_all.at[group_rows(peer(distance))],
            dst_ref=attn_got.at[distance - 1],
            send_sem=attn_send.at[distance - 1],
            recv_sem=attn_recv.at[distance - 1],
            device_id={"tp": peer(distance)},
            device_id_type=MESH,
        )

    def down_copy(distance, direction, step):
        block = shard_req(direction, step) * 2 + direction
        sem_index = ((distance - 1) * 2 + direction) * ring_size + step
        return pltpu.make_async_remote_copy(
            src_ref=down_part.at[block, group_rows(peer(distance))],
            dst_ref=down_got.at[distance - 1, block],
            send_sem=down_send.at[sem_index],
            recv_sem=down_recv.at[sem_index],
            device_id={"tp": peer(distance)},
            device_id_type=MESH,
        )

    def rows_dot(a, b):
        return lax.dot_general(
            a, b, (((1,), (1,)), ((), ())), preferred_element_type=jnp.float32
        )

    barrier = pltpu.get_barrier_semaphore()
    for neighbour in (left, right):
        pl.semaphore_signal(
            barrier, inc=1, device_id={"req": neighbour}, device_id_type=MESH
        )
    for distance in range(1, group_size):
        pl.semaphore_signal(
            barrier, inc=1, device_id={"tp": peer(distance)}, device_id_type=MESH
        )
    pl.semaphore_wait(barrier, 1 + group_size)

    begin(mix_phase)
    for index in range(4):
        own_copy(index).start()
    normed_all[group_rows(my_tp), :] = normed(tokens_ref[...], norm_gain_ref[...])
    for distance in range(1, group_size):
        gather_copy(normed_all, gather_send, gather_recv, distance).start()

    length = length_ref[0]
    row_ids = lax.broadcasted_iota(jnp.int32, (window, window), 0)
    col_ids = lax.broadcasted_iota(jnp.int32, (window, window), 1)
    slot_order = ((col_ids - row_ids - length) & (window - 1)) == 0
    slot_order = jnp.where(slot_order, 1.0, 0.0).astype(jnp.bfloat16)
    slot_back = ((row_ids - col_ids - length - row_total) & (window - 1)) == 0
    slot_back = jnp.where(slot_back, 1.0, 0.0).astype(jnp.bfloat16)
    spread_one = spread_ref[0:feat_width, 0:wide]
    for part, rows_ref in ((0, key_rows), (1, value_rows)):
        earlier = jnp.dot(slot_order, cache_ref[part], preferred_element_type=jnp.float32)
        rows_ref[0:window, :] = jnp.dot(
            earlier.astype(jnp.bfloat16), spread_one, preferred_element_type=jnp.float32
        ).astype(jnp.bfloat16)

    ticks(mix_phase, 1, last + 1)
    begin(ffn_phase)
    for distance in range(1, group_size):
        gather_arrived(normed_all, gather_send, gather_recv, distance)
    own_copy(0).wait()
    own_copy(1).wait()
    finish(mix_phase)

    @pl.loop(0, mix_all.shape[1] // 256)
    def _(tile):
        cols = pl.ds(pl.multiple_of(tile * 256, 256), 256)
        shared[:, cols] = jnp.dot(
            normed_all[...], mix_all[:, cols], preferred_element_type=jnp.float32
        ).astype(jnp.bfloat16)

    block_rows = 128
    key_count = block_rows + window
    score_scale = 1.0 / math.sqrt(head_size)

    def attend(block):
        begin_row = pl.multiple_of(block * block_rows, 128)
        rows = pl.ds(begin_row, block_rows)
        left_half = jnp.dot(
            shared[rows, 0 : 2 * feat_width], spread_ref[...], preferred_element_type=jnp.float32
        ).astype(jnp.bfloat16)
        right_half = jnp.dot(
            shared[rows, 2 * feat_width : 4 * feat_width],
            spread_ref[...],
            preferred_element_type=jnp.float32,
        )
        new_rows = pl.ds(pl.multiple_of(block * block_rows + window, 64), block_rows)
        key_rows[new_rows, :] = left_half[:, wide:]
        value_rows[new_rows, :] = right_half[:, :wide].astype(jnp.bfloat16)
        keys = key_rows[pl.ds(begin_row, key_count), :]
        values = value_rows[pl.ds(begin_row, key_count), :]
        query_ids = lax.broadcasted_iota(jnp.int32, (block_rows, key_count), 0)
        key_ids = lax.broadcasted_iota(jnp.int32, (block_rows, key_count), 1)
        usable = (
            (key_ids > query_ids)
            & (key_ids <= query_ids + window)
            & (key_ids + begin_row >= window - length)
        )
        attended = []
        for head in range(head_count):
            cols = slice(head * 128, head * 128 + 128)
            scores = rows_dot(left_half[:, cols], keys[:, cols]) * score_scale
            scores = jnp.where(usable, scores, -1e30)
            exponent = jnp.exp(scores - jnp.max(scores, axis=-1, keepdims=True))
            weights = exponent / jnp.sum(exponent, axis=-1, keepdims=True)
            attended.append(
                jnp.dot(
                    weights.astype(jnp.bfloat16),
                    values[:, cols],
                    preferred_element_type=jnp.float32,
                )
            )
        attended = jnp.concatenate(attended, axis=1)
        live_ids = lax.broadcasted_iota(jnp.int32, (key_count, wide), 0) + begin_row
        live = jnp.where(live_ids >= window - length, values.astype(jnp.float32), 0.0)
        tap_count = taps_ref.shape[0]
        convolved = jnp.zeros((block_rows, wide), jnp.float32)
        for tap in range(tap_count):
            shift = tap_count - 1 - tap
            moved = pltpu.roll(live, shift, 0) if shift else live
            convolved = convolved + taps_ref[tap : tap + 1, :] * moved[window:, :]
        gates = right_half[:, wide:]
        heads = (attended + gates * convolved).astype(jnp.bfloat16)
        mixed[rows, :] = rows_dot(heads, spread_one).astype(jnp.bfloat16)

    block_total = row_total // block_rows
    pl.loop(0, block_total // 2)(attend)
    tick(ffn_phase, 1)
    pl.loop(block_total // 2, block_total)(attend)

    for part, rows_ref in ((0, key_rows), (1, value_rows)):
        tail = jnp.dot(
            slot_back,
            rows_ref[row_total : row_total + window, :],
            preferred_element_type=jnp.float32,
        )
        renewed_ref[part] = rows_dot(tail.astype(jnp.bfloat16), spread_one).astype(jnp.bfloat16)

    for distance in range(1, group_size):
        gather_copy(normed_all, gather_send, gather_recv, distance).wait_send()
    for distance in list(range(1, group_size)) + [0]:
        rows = group_rows(peer(distance))
        normed_all[rows, :] = rows_dot(mixed[rows, :], out_all[...]).astype(jnp.bfloat16)
        if distance:
            attn_copy(distance).start()

    ticks(ffn_phase, 2, min(5, last + 1))
    attn_sum = normed_all[group_rows(my_tp), :].astype(jnp.float32)
    for distance in range(1, group_size):
        attn_copy(distance).wait_recv()
        attn_sum = attn_sum + attn_got[distance - 1].astype(jnp.float32)
    residual = (tokens_ref[...].astype(jnp.float32) + attn_sum).astype(jnp.bfloat16)
    residual_ref[...] = residual
    ffn_in_all[group_rows(my_tp), :] = normed(residual, ffn_gain_ref[...])
    for distance in range(1, group_size):
        gather_copy(ffn_in_all, ffn_send, ffn_recv, distance).start()

    ticks(ffn_phase, min(5, last + 1), last + 1)
    begin(down_phase)
    for distance in range(1, group_size):
        gather_arrived(ffn_in_all, ffn_send, ffn_recv, distance)
    own_copy(2).wait()
    own_copy(3).wait()
    finish(ffn_phase)

    tile_count = hidden // 256
    early = 1 + tile_count // 3

    @pl.loop(0, tile_count)
    def _(tile):
        begin_col = pl.multiple_of(tile * 256, 256)
        gate = jnp.dot(
            ffn_in_all[...], ffn_all[:, pl.ds(begin_col, 256)], preferred_element_type=jnp.float32
        )
        up = jnp.dot(
            ffn_in_all[...],
            ffn_all[:, pl.ds(pl.multiple_of(hidden + begin_col, 256), 256)],
            preferred_element_type=jnp.float32,
        )
        activated = gate / (1.0 + jnp.exp(-gate)) * up
        shared[:, pl.ds(begin_col, 256)] = activated.astype(jnp.bfloat16)

        @pl.when(tile % 3 == 2)
        def _():
            tick(down_phase, tile // 3 + 1)

    def consume(step):
        for direction in range(2):
            block = shard_req(direction, step) * 2 + direction
            down_part[block] = rows_dot(
                shared[...], down_all[pl.ds(half_begin(direction, step), half), :]
            ).astype(jnp.bfloat16)
            for distance in range(1, group_size):
                down_copy(distance, direction, step).start()

    pl.loop(0, early)(consume)

    @pl.loop(early, last + 1)
    def _(step):
        tick(down_phase, step)
        consume(step)

    finish(down_phase)
    consume(ring_size - 1)

    @pl.loop(0, ring_size)
    def _(step):
        for direction in range(2):
            block = shard_req(direction, step) * 2 + direction
            total = down_part[block, group_rows(my_tp), :].astype(jnp.float32)
            for distance in range(1, group_size):
                down_copy(distance, direction, step).wait_recv()
                total = total + down_got[distance - 1, block].astype(jnp.float32)
            ffn_sum_ref[block] = total

    for stream in range(len(streams)):
        for direction in range(2):
            ring_copy(stream, direction, 0, True).wait_send()

            @pl.loop(1, last + 1)
            def _(step):
                ring_copy(stream, direction, step, False).wait_send()

    for distance in range(1, group_size):
        attn_copy(distance).wait_send()
        gather_copy(ffn_in_all, ffn_send, ffn_recv, distance).wait_send()

        @pl.loop(0, ring_size)
        def _(step):
            for direction in range(2):
                down_copy(distance, direction, step).wait_send()


def fused(
    ring_size,
    group_size,
    tokens,
    norm_gain,
    ffn_gain,
    mix_weight,
    out_weight,
    ffn_weight,
    down_weight,
    conv_taps,
    past_cache,
    cached_len,
):
    own_rows, width = tokens.shape
    row_total = own_rows * group_size
    shard_rows, _, feat_width = mix_weight.shape
    hidden = ffn_weight.shape[2]
    half = shard_rows // 2
    head_count = feat_width // HD
    wide = head_count * 128
    window = past_cache.shape[2]

    def widen(array):
        heads = array.reshape(array.shape[0], head_count, HD)
        return jnp.pad(heads, ((0, 0), (0, 0), (0, 128 - HD))).reshape(array.shape[0], wide)

    spread_table = np.zeros((2, feat_width, 2, head_count, 128), np.float32)
    for part in range(2):
        for feature in range(feat_width):
            spread_table[part, feature, part, feature // HD, feature % HD] = 1.0
    spread = jnp.asarray(spread_table.reshape(2 * feat_width, 2 * wide), jnp.bfloat16)
    bf16, f32 = jnp.bfloat16, jnp.float32
    in_vmem = pl.BlockSpec(memory_space=pltpu.VMEM)
    in_place = pl.BlockSpec(memory_space=pl.ANY)
    peers = group_size - 1
    ring_sems = pltpu.SemaphoreType.DMA((7 * 2 * (ring_size - 1),))
    peer_sems = pltpu.SemaphoreType.DMA((peers,))
    down_sems = pltpu.SemaphoreType.DMA((peers * 2 * ring_size,))
    ffn_sum, residual, renewed = pl.pallas_call(
        functools.partial(layer_kernel, ring_size, group_size, window, head_count, HD),
        out_shape=(
            jax.ShapeDtypeStruct((2 * ring_size, own_rows, half), f32),
            jax.ShapeDtypeStruct((own_rows, width), bf16),
            jax.ShapeDtypeStruct((2, window, feat_width), bf16),
        ),
        in_specs=[in_vmem] * 5
        + [pl.BlockSpec(memory_space=pltpu.SMEM)]
        + [in_vmem]
        + [in_place] * 4,
        out_specs=(in_vmem,) * 3,
        scratch_shapes=[
            pltpu.VMEM((width, 4 * feat_width), bf16),
            pltpu.VMEM((width, feat_width), bf16),
            pltpu.VMEM((width, 2 * hidden), bf16),
            pltpu.VMEM((width, hidden), bf16),
            pltpu.VMEM((row_total, width), bf16),
            pltpu.VMEM((row_total, width), bf16),
            pltpu.VMEM((window + row_total, wide), bf16),
            pltpu.VMEM((window + row_total, wide), bf16),
            pltpu.VMEM((row_total, feat_width), bf16),
            pltpu.VMEM((peers, own_rows, width), bf16),
            pltpu.VMEM((row_total, hidden), bf16),
            pltpu.VMEM((2 * ring_size, row_total, half), bf16),
            pltpu.VMEM((peers, 2 * ring_size, own_rows, half), bf16),
            ring_sems,
            ring_sems,
            pltpu.SemaphoreType.DMA((4,)),
            peer_sems,
            peer_sems,
            peer_sems,
            peer_sems,
            peer_sems,
            peer_sems,
            down_sems,
            down_sems,
        ],
        compiler_params=pltpu.CompilerParams(
            collective_id=0, has_side_effects=True, vmem_limit_bytes=63 * 1024 * 1024
        ),
    )(
        tokens,
        norm_gain.reshape(1, width),
        ffn_gain.reshape(1, width),
        widen(conv_taps),
        past_cache[0],
        cached_len,
        spread,
        mix_weight.reshape(shard_rows, 4 * feat_width),
        out_weight.T,
        ffn_weight.reshape(shard_rows, 2 * hidden),
        down_weight.T,
    )
    ffn_part = jnp.transpose(ffn_sum, (1, 0, 2)).reshape(own_rows, width)
    layer_out = (residual.astype(f32) + ffn_part).astype(bf16)
    return (layer_out, renewed[None])


def solution(mesh):
    in_specs = (
        P(("req", "tp"), None),
        P(),
        P(),
        P("req", None, "tp"),
        P("tp", "req"),
        P("req", None, "tp"),
        P("tp", "req"),
        P(None, "tp"),
        P("req", None, None, "tp"),
        P("req"),
    )
    out_specs = (P(("req", "tp"), None), P("req", None, None, "tp"))
    ring_size, group_size = mesh.shape["req"], mesh.shape["tp"]

    def device_layer(*args):
        tokens, mix_weight, ffn_weight = args[0], args[3], args[5]
        shard_rows, _, feat_width = mix_weight.shape
        fits = (
            ring_size > 5
            and ring_size % 2 == 0
            and group_size == 4
            and shard_rows % 32 == 0
            and feat_width % (HD * 4) == 0
            and feat_width * 4 == ffn_weight.shape[2]
            and ffn_weight.shape[2] % 256 == 0
            and tokens.shape[0] == 256
        )
        if fits:
            return fused(ring_size, group_size, *args)
        return local(*args)

    return jax.shard_map(
        device_layer, mesh=mesh, in_specs=in_specs, out_specs=out_specs, check_vma=False
    )
```

```python
import functools
import math

import jax
import jax.numpy as jnp
import numpy as np
from jax import lax
from jax.experimental import pallas as pl
from jax.experimental.pallas import tpu as pltpu
from jax.sharding import PartitionSpec as P

HD = 112
WIN = 64


def normed(row_vals, gain):
    floats = row_vals.astype(jnp.float32)
    scaled = floats * lax.rsqrt(jnp.mean(floats * floats, axis=-1, keepdims=True) + 1e-05)
    return (scaled * gain).astype(jnp.bfloat16)


def window_attend(queries, key_rows, value_rows, length, window):
    row_count, head_count, head_size = queries.shape
    block_rows = min(512, row_count)
    score_scale = 1.0 / math.sqrt(head_size)

    def one_block(block_index):
        begin_row = block_index * block_rows
        query_block = lax.dynamic_slice_in_dim(queries, begin_row, block_rows, 0)
        key_block = lax.dynamic_slice_in_dim(key_rows, begin_row, block_rows + window, 0)
        value_block = lax.dynamic_slice_in_dim(value_rows, begin_row, block_rows + window, 0)
        scores = (
            jnp.einsum("qhd,khd->hqk", query_block, key_block, preferred_element_type=jnp.float32)
            * score_scale
        )
        row_ids = begin_row + jnp.arange(block_rows, dtype=jnp.int32)[:, None]
        col_ids = begin_row + jnp.arange(block_rows + window, dtype=jnp.int32)[None, :]
        usable = (col_ids > row_ids) & (col_ids <= row_ids + window) & (col_ids >= window - length)
        scores = jnp.where(usable[None], scores, -1e30)
        row_max = jnp.max(scores, axis=-1, keepdims=True)
        exponent = jnp.exp(scores - row_max)
        weights = (exponent / jnp.sum(exponent, axis=-1, keepdims=True)).astype(jnp.bfloat16)
        return jnp.einsum("hqk,khd->qhd", weights, value_block, preferred_element_type=jnp.float32)

    blocks = lax.map(one_block, jnp.arange(row_count // block_rows, dtype=jnp.int32))
    return blocks.reshape(row_count, head_count, head_size)


def mix_request(projected, cache_rows, length, tap_table, window, head_size):
    row_count, feat_width = (projected.shape[0], projected.shape[2])
    time_order = (length + jnp.arange(window, dtype=jnp.int32)) % window
    earlier = cache_rows[:, time_order]
    key_rows = jnp.concatenate([earlier[0], projected[:, 1]], axis=0)
    value_rows = jnp.concatenate([earlier[1], projected[:, 2]], axis=0)
    head_count = feat_width // head_size
    attended = window_attend(
        projected[:, 0].reshape(row_count, head_count, head_size),
        key_rows.reshape(-1, head_count, head_size),
        value_rows.reshape(-1, head_count, head_size),
        length,
        window,
    ).reshape(row_count, feat_width)
    positions = jnp.arange(window + row_count, dtype=jnp.int32)
    alive_mask = (positions >= window - length)[:, None]
    masked_values = jnp.where(alive_mask, value_rows.astype(jnp.float32), jnp.float32(0.0))
    tap_count = tap_table.shape[0]
    convolved = jnp.zeros((row_count, feat_width), jnp.float32)
    for tap_index in range(tap_count):
        begin_row = window - (tap_count - 1) + tap_index
        convolved = (
            convolved + tap_table[tap_index] * masked_values[begin_row : begin_row + row_count]
        )
    mixed_heads = (attended + projected[:, 3].astype(jnp.float32) * convolved).astype(jnp.bfloat16)
    slot_source = (
        row_count - window + (jnp.arange(window, dtype=jnp.int32) - length - row_count) % window
    )
    renewed = jnp.stack([projected[:, 1], projected[:, 2]])[:, slot_source]
    return (mixed_heads, renewed)


def add_rows(left, shard_piece):
    return jnp.dot(
        left, shard_piece.reshape(shard_piece.shape[0], -1), preferred_element_type=jnp.float32
    )


def local(
    tokens,
    norm_gain,
    ffn_gain,
    mix_weight,
    out_weight,
    ffn_weight,
    down_weight,
    conv_taps,
    past_cache,
    cached_len,
):
    feat_width = mix_weight.shape[2]
    ffn_width = ffn_weight.shape[2]
    normed_all = lax.all_gather(normed(tokens, norm_gain), "tp", axis=0, tiled=True)
    row_total = normed_all.shape[0]
    projected = add_rows(normed_all, lax.all_gather(mix_weight, "req", axis=0, tiled=True))
    projected = projected.astype(jnp.bfloat16).reshape(row_total, 4, feat_width)
    mixed_heads, renewed = mix_request(projected, past_cache[0], cached_len[0], conv_taps, WIN, HD)
    out_columns = lax.all_gather(out_weight, "req", axis=1, tiled=True)
    attn_part = lax.psum_scatter(
        jnp.dot(mixed_heads, out_columns, preferred_element_type=jnp.float32).astype(jnp.bfloat16),
        "tp",
        scatter_dimension=0,
        tiled=True,
    ).astype(jnp.float32)
    residual = (tokens.astype(jnp.float32) + attn_part).astype(jnp.bfloat16)
    ffn_in = lax.all_gather(normed(residual, ffn_gain), "tp", axis=0, tiled=True)
    gate_up = add_rows(ffn_in, lax.all_gather(ffn_weight, "req", axis=0, tiled=True))
    down_columns = lax.all_gather(down_weight, "req", axis=1, tiled=True)
    activated = (jax.nn.silu(gate_up[:, :ffn_width]) * gate_up[:, ffn_width:]).astype(jnp.bfloat16)
    ffn_part = lax.psum_scatter(
        jnp.dot(activated, down_columns, preferred_element_type=jnp.float32).astype(jnp.bfloat16),
        "tp",
        scatter_dimension=0,
        tiled=True,
    ).astype(jnp.float32)
    layer_out = (residual.astype(jnp.float32) + ffn_part).astype(jnp.bfloat16)
    return (layer_out, renewed[None])

MESH = pl.DeviceIdType.MESH


def ring_spot(req_index, ring_size):
    z_index, y_index = req_index // 2, req_index % 2
    return z_index * (1 - y_index) + (ring_size - 1 - z_index) * y_index


def spot_req(spot, ring_size):
    side = spot // (ring_size // 2)
    return 2 * (spot * (1 - side) + (ring_size - 1 - spot) * side) + side


def layer_kernel(
    ring_size,
    group_size,
    window,
    head_count,
    head_size,
    tokens_ref,
    norm_gain_ref,
    ffn_gain_ref,
    taps_ref,
    cache_ref,
    length_ref,
    spread_ref,
    mix_ref,
    out_ref,
    ffn_ref,
    down_ref,
    ffn_sum_ref,
    residual_ref,
    renewed_ref,
    mix_all,
    out_all,
    ffn_all,
    down_all,
    normed_all,
    ffn_in_all,
    key_rows,
    value_rows,
    mixed,
    attn_got,
    shared,
    down_part,
    down_got,
    ring_send,
    ring_recv,
    own_sem,
    gather_send,
    gather_recv,
    attn_send,
    attn_recv,
    ffn_send,
    ffn_recv,
    down_send,
    down_recv,
):
    my_req, my_tp = lax.axis_index("req"), lax.axis_index("tp")
    spot = ring_spot(my_req, ring_size)
    right = spot_req((spot + 1) % ring_size, ring_size)
    left = spot_req((spot + ring_size - 1) % ring_size, ring_size)
    own_rows, width = tokens_ref.shape
    row_total = own_rows * group_size
    shard_rows = mix_ref.shape[0]
    half = shard_rows // 2
    feat_width = out_all.shape[1]
    hidden = ffn_all.shape[1] // 2
    half_cols = mix_ref.shape[1] // 2
    wide = head_count * 128
    last = ring_size - 2

    tile_count = hidden // 256
    early_tiles = (tile_count + 1) // 2
    early_hidden = early_tiles * 256

    streams = [
        (out_ref, out_all, 0, feat_width),
        (mix_ref, mix_all, 0, half_cols),
        (mix_ref, mix_all, half_cols, half_cols),
        (ffn_ref, ffn_all, 0, early_hidden),
        (ffn_ref, ffn_all, hidden, early_hidden),
        (ffn_ref, ffn_all, early_hidden, hidden - early_hidden),
        (ffn_ref, ffn_all, hidden + early_hidden, hidden - early_hidden),
        (down_ref, down_all, 0, hidden // 2),
        (down_ref, down_all, hidden // 2, hidden // 2),
    ]
    mix_phase, early_phase, late_phase, down_phase = (0, 1, 2), (3, 4), (5, 6), (7, 8)

    def shard_req(direction, step):
        if direction == 0:
            return spot_req((spot + ring_size - step) % ring_size, ring_size)
        return spot_req((spot + step) % ring_size, ring_size)

    def half_begin(direction, step):
        return pl.multiple_of(shard_req(direction, step) * shard_rows + direction * half, 16)

    def ring_copy(stream, direction, step, first):
        source, whole, col_begin, col_count = streams[stream]
        cols = pl.ds(col_begin, col_count)
        place = whole.at[pl.ds(half_begin(direction, step), half), cols]
        sem_index = (stream * 2 + direction) * (ring_size - 1) + step
        return pltpu.make_async_remote_copy(
            src_ref=source.at[pl.ds(direction * half, half), cols] if first else place,
            dst_ref=place,
            send_sem=ring_send.at[sem_index],
            recv_sem=ring_recv.at[sem_index],
            device_id={"req": left if direction else right},
            device_id_type=MESH,
        )

    def ring_arrived(stream, direction, step):
        _, whole, col_begin, col_count = streams[stream]
        place = whole.at[
            pl.ds(half_begin(direction, step + 1), half), pl.ds(col_begin, col_count)
        ]
        sem_index = (stream * 2 + direction) * (ring_size - 1) + step
        pltpu.make_async_remote_copy(
            src_ref=place,
            dst_ref=place,
            send_sem=ring_send.at[sem_index],
            recv_sem=ring_recv.at[sem_index],
            device_id={"req": left if direction else right},
            device_id_type=MESH,
        ).wait_recv()

    def begin(phase):
        for stream in phase:
            for direction in range(2):
                ring_copy(stream, direction, 0, True).start()

    def tick(phase, step):
        for stream in phase:
            for direction in range(2):
                ring_arrived(stream, direction, step - 1)
                ring_copy(stream, direction, step, False).start()

    def ticks(phase, low, high):
        @pl.loop(low, high)
        def _(step):
            tick(phase, step)

    def finish(phase):
        for stream in phase:
            for direction in range(2):
                ring_arrived(stream, direction, last)

    def own_copy(index):
        source, whole = ((mix_ref, mix_all), (out_ref, out_all), (ffn_ref, ffn_all), (down_ref, down_all))[index]
        begin_row = pl.multiple_of(my_req * shard_rows, 16)
        return pltpu.make_async_copy(
            source, whole.at[pl.ds(begin_row, shard_rows)], own_sem.at[index]
        )

    def peer(distance):
        return (my_tp + distance) % group_size

    def group_rows(member):
        return pl.ds(pl.multiple_of(member * own_rows, 16), own_rows)

    sibling = my_tp + 1 - 2 * (my_tp % 2)
    across = peer(2)
    diagonal = (sibling + 2) % group_size

    def peer_copy(source, target, sends, recvs, index, member):
        return pltpu.make_async_remote_copy(
            src_ref=source,
            dst_ref=target,
            send_sem=sends.at[index],
            recv_sem=recvs.at[index],
            device_id={"tp": member},
            device_id_type=MESH,
        )

    def gather_copy(whole, sends, recvs, index):
        rows = whole.at[group_rows(across if index == 2 else my_tp)]
        return peer_copy(rows, rows, sends, recvs, index, sibling if index else across)

    def gather_arrived(whole, sends, recvs, index):
        rows = whole.at[group_rows((across, sibling, diagonal)[index])]
        peer_copy(rows, rows, sends, recvs, index, sibling if index else across).wait_recv()

    def attn_copy(index):
        rows = normed_all.at[group_rows((sibling, diagonal, across)[index])]
        return peer_copy(
            rows, attn_got.at[index], attn_send, attn_recv, index, across if index == 2 else sibling
        )

    def down_copy(distance, direction, step):
        block = shard_req(direction, step) * 2 + direction
        sem_index = ((distance - 1) * 2 + direction) * ring_size + step
        return pltpu.make_async_remote_copy(
            src_ref=down_part.at[block, group_rows(peer(distance))],
            dst_ref=down_got.at[distance - 1, block],
            send_sem=down_send.at[sem_index],
            recv_sem=down_recv.at[sem_index],
            device_id={"tp": peer(distance)},
            device_id_type=MESH,
        )

    def rows_dot(a, b):
        return lax.dot_general(
            a, b, (((1,), (1,)), ((), ())), preferred_element_type=jnp.float32
        )

    barrier = pltpu.get_barrier_semaphore()
    for neighbour in (left, right):
        pl.semaphore_signal(
            barrier, inc=1, device_id={"req": neighbour}, device_id_type=MESH
        )
    for distance in range(1, group_size):
        pl.semaphore_signal(
            barrier, inc=1, device_id={"tp": peer(distance)}, device_id_type=MESH
        )
    pl.semaphore_wait(barrier, 1 + group_size)

    begin(mix_phase)
    for index in range(4):
        own_copy(index).start()
    normed_all[group_rows(my_tp), :] = normed(tokens_ref[...], norm_gain_ref[...])
    for index in range(2):
        gather_copy(normed_all, gather_send, gather_recv, index).start()

    length = length_ref[0]
    row_ids = lax.broadcasted_iota(jnp.int32, (window, window), 0)
    col_ids = lax.broadcasted_iota(jnp.int32, (window, window), 1)
    slot_order = ((col_ids - row_ids - length) & (window - 1)) == 0
    slot_order = jnp.where(slot_order, 1.0, 0.0).astype(jnp.bfloat16)
    slot_back = ((row_ids - col_ids - length - row_total) & (window - 1)) == 0
    slot_back = jnp.where(slot_back, 1.0, 0.0).astype(jnp.bfloat16)
    spread_one = spread_ref[0:feat_width, 0:wide]
    for part, rows_ref in ((0, key_rows), (1, value_rows)):
        earlier = jnp.dot(slot_order, cache_ref[part], preferred_element_type=jnp.float32)
        rows_ref[0:window, :] = jnp.dot(
            earlier.astype(jnp.bfloat16), spread_one, preferred_element_type=jnp.float32
        ).astype(jnp.bfloat16)

    ticks(mix_phase, 1, 4)
    gather_arrived(normed_all, gather_send, gather_recv, 0)
    gather_copy(normed_all, gather_send, gather_recv, 2).start()
    ticks(mix_phase, 4, last + 1)
    begin(early_phase)
    for index in (1, 2):
        gather_arrived(normed_all, gather_send, gather_recv, index)
    own_copy(0).wait()
    own_copy(1).wait()
    finish(mix_phase)

    @pl.loop(0, mix_all.shape[1] // 256)
    def _(tile):
        cols = pl.ds(pl.multiple_of(tile * 256, 256), 256)
        shared[:, cols] = jnp.dot(
            normed_all[...], mix_all[:, cols], preferred_element_type=jnp.float32
        ).astype(jnp.bfloat16)

    block_rows = 128
    key_count = block_rows + window
    score_scale = 1.0 / math.sqrt(head_size)

    def attend(block):
        begin_row = pl.multiple_of(block * block_rows, 128)
        rows = pl.ds(begin_row, block_rows)
        left_half = jnp.dot(
            shared[rows, 0 : 2 * feat_width], spread_ref[...], preferred_element_type=jnp.float32
        ).astype(jnp.bfloat16)
        right_half = jnp.dot(
            shared[rows, 2 * feat_width : 4 * feat_width],
            spread_ref[...],
            preferred_element_type=jnp.float32,
        )
        new_rows = pl.ds(pl.multiple_of(block * block_rows + window, 64), block_rows)
        key_rows[new_rows, :] = left_half[:, wide:]
        value_rows[new_rows, :] = right_half[:, :wide].astype(jnp.bfloat16)
        keys = key_rows[pl.ds(begin_row, key_count), :]
        values = value_rows[pl.ds(begin_row, key_count), :]
        query_ids = lax.broadcasted_iota(jnp.int32, (block_rows, key_count), 0)
        key_ids = lax.broadcasted_iota(jnp.int32, (block_rows, key_count), 1)
        usable = (
            (key_ids > query_ids)
            & (key_ids <= query_ids + window)
            & (key_ids + begin_row >= window - length)
        )
        attended = []
        for head in range(head_count):
            cols = slice(head * 128, head * 128 + 128)
            scores = rows_dot(left_half[:, cols], keys[:, cols]) * score_scale
            scores = jnp.where(usable, scores, -1e30)
            exponent = jnp.exp(scores - jnp.max(scores, axis=-1, keepdims=True))
            weights = exponent / jnp.sum(exponent, axis=-1, keepdims=True)
            attended.append(
                jnp.dot(
                    weights.astype(jnp.bfloat16),
                    values[:, cols],
                    preferred_element_type=jnp.float32,
                )
            )
        attended = jnp.concatenate(attended, axis=1)
        live_ids = lax.broadcasted_iota(jnp.int32, (key_count, wide), 0) + begin_row
        live = jnp.where(live_ids >= window - length, values.astype(jnp.float32), 0.0)
        tap_count = taps_ref.shape[0]
        convolved = jnp.zeros((block_rows, wide), jnp.float32)
        for tap in range(tap_count):
            shift = tap_count - 1 - tap
            moved = pltpu.roll(live, shift, 0) if shift else live
            convolved = convolved + taps_ref[tap : tap + 1, :] * moved[window:, :]
        gates = right_half[:, wide:]
        heads = (attended + gates * convolved).astype(jnp.bfloat16)
        mixed[rows, :] = rows_dot(heads, spread_one).astype(jnp.bfloat16)

    block_total = row_total // block_rows
    tick(early_phase, 1)

    @pl.loop(0, block_total)
    def _(block):
        attend(block)

        @pl.when(block % 3 == 2)
        def _():
            tick(early_phase, 2 + block // 3)

    for part, rows_ref in ((0, key_rows), (1, value_rows)):
        tail = jnp.dot(
            slot_back,
            rows_ref[row_total : row_total + window, :],
            preferred_element_type=jnp.float32,
        )
        renewed_ref[part] = rows_dot(tail.astype(jnp.bfloat16), spread_one).astype(jnp.bfloat16)

    for index in range(3):
        gather_copy(normed_all, gather_send, gather_recv, index).wait_send()
    tick(early_phase, 4)
    for index, member in enumerate((sibling, diagonal, across, my_tp)):
        rows = group_rows(member)
        normed_all[rows, :] = rows_dot(mixed[rows, :], out_all[...]).astype(jnp.bfloat16)
        if index < 2:
            attn_copy(index).start()
    ticks(early_phase, 5, last)
    attn_copy(1).wait_recv()
    rows = group_rows(across)
    normed_all[rows, :] = (
        normed_all[rows, :].astype(jnp.float32) + attn_got[1].astype(jnp.float32)
    ).astype(jnp.bfloat16)
    attn_copy(2).start()
    tick(early_phase, last)
    begin(late_phase)
    own_copy(2).wait()
    own_copy(3).wait()
    finish(early_phase)
    attn_sum = normed_all[group_rows(my_tp), :].astype(jnp.float32)
    for index in (0, 2):
        attn_copy(index).wait_recv()
        attn_sum = attn_sum + attn_got[index].astype(jnp.float32)
    residual = (tokens_ref[...].astype(jnp.float32) + attn_sum).astype(jnp.bfloat16)
    residual_ref[...] = residual
    ffn_in_all[group_rows(my_tp), :] = normed(residual, ffn_gain_ref[...])
    for index in range(2):
        gather_copy(ffn_in_all, ffn_send, ffn_recv, index).start()

    ticks(late_phase, 1, 4)
    gather_arrived(ffn_in_all, ffn_send, ffn_recv, 0)
    gather_copy(ffn_in_all, ffn_send, ffn_recv, 2).start()
    for index in (1, 2):
        gather_arrived(ffn_in_all, ffn_send, ffn_recv, index)

    def activate(tile):
        begin_col = pl.multiple_of(tile * 256, 256)
        gate = jnp.dot(
            ffn_in_all[...], ffn_all[:, pl.ds(begin_col, 256)], preferred_element_type=jnp.float32
        )
        up = jnp.dot(
            ffn_in_all[...],
            ffn_all[:, pl.ds(pl.multiple_of(hidden + begin_col, 256), 256)],
            preferred_element_type=jnp.float32,
        )
        activated = gate / (1.0 + jnp.exp(-gate)) * up
        shared[:, pl.ds(begin_col, 256)] = activated.astype(jnp.bfloat16)

    @pl.loop(0, early_tiles)
    def _(tile):
        activate(tile)

        @pl.when(tile + 4 <= last)
        def _():
            tick(late_phase, tile + 4)

    ticks(late_phase, 4 + early_tiles, last + 1)
    begin(down_phase)
    finish(late_phase)

    @pl.loop(early_tiles, tile_count)
    def _(tile):
        activate(tile)

        @pl.when(tile == early_tiles + 1)
        def _():
            tick(down_phase, 1)

    def consume(step):
        for direction in range(2):
            block = shard_req(direction, step) * 2 + direction
            down_part[block] = rows_dot(
                shared[...], down_all[pl.ds(half_begin(direction, step), half), :]
            ).astype(jnp.bfloat16)
            for distance in range(1, group_size):
                down_copy(distance, direction, step).start()

    pl.loop(0, 2)(consume)

    @pl.loop(2, last + 1)
    def _(step):
        tick(down_phase, step)
        consume(step)

    finish(down_phase)
    consume(ring_size - 1)

    @pl.loop(0, ring_size)
    def _(step):
        for direction in range(2):
            block = shard_req(direction, step) * 2 + direction
            total = down_part[block, group_rows(my_tp), :].astype(jnp.float32)
            for distance in range(1, group_size):
                down_copy(distance, direction, step).wait_recv()
                total = total + down_got[distance - 1, block].astype(jnp.float32)
            ffn_sum_ref[block] = total

    for stream in range(len(streams)):
        for direction in range(2):
            ring_copy(stream, direction, 0, True).wait_send()

            @pl.loop(1, last + 1)
            def _(step):
                ring_copy(stream, direction, step, False).wait_send()

    for index in range(3):
        attn_copy(index).wait_send()
        gather_copy(ffn_in_all, ffn_send, ffn_recv, index).wait_send()
    for distance in range(1, group_size):

        @pl.loop(0, ring_size)
        def _(step):
            for direction in range(2):
                down_copy(distance, direction, step).wait_send()


def fused(
    ring_size,
    group_size,
    tokens,
    norm_gain,
    ffn_gain,
    mix_weight,
    out_weight,
    ffn_weight,
    down_weight,
    conv_taps,
    past_cache,
    cached_len,
):
    own_rows, width = tokens.shape
    row_total = own_rows * group_size
    shard_rows, _, feat_width = mix_weight.shape
    hidden = ffn_weight.shape[2]
    half = shard_rows // 2
    head_count = feat_width // HD
    wide = head_count * 128
    window = past_cache.shape[2]

    def widen(array):
        heads = array.reshape(array.shape[0], head_count, HD)
        return jnp.pad(heads, ((0, 0), (0, 0), (0, 128 - HD))).reshape(array.shape[0], wide)

    spread_table = np.zeros((2, feat_width, 2, head_count, 128), np.float32)
    for part in range(2):
        for feature in range(feat_width):
            spread_table[part, feature, part, feature // HD, feature % HD] = 1.0
    spread = jnp.asarray(spread_table.reshape(2 * feat_width, 2 * wide), jnp.bfloat16)
    bf16, f32 = jnp.bfloat16, jnp.float32
    in_vmem = pl.BlockSpec(memory_space=pltpu.VMEM)
    in_place = pl.BlockSpec(memory_space=pl.ANY)
    peers = group_size - 1
    ring_sems = pltpu.SemaphoreType.DMA((9 * 2 * (ring_size - 1),))
    peer_sems = pltpu.SemaphoreType.DMA((peers,))
    down_sems = pltpu.SemaphoreType.DMA((peers * 2 * ring_size,))
    ffn_sum, residual, renewed = pl.pallas_call(
        functools.partial(layer_kernel, ring_size, group_size, window, head_count, HD),
        out_shape=(
            jax.ShapeDtypeStruct((2 * ring_size, own_rows, half), f32),
            jax.ShapeDtypeStruct((own_rows, width), bf16),
            jax.ShapeDtypeStruct((2, window, feat_width), bf16),
        ),
        in_specs=[in_vmem] * 5
        + [pl.BlockSpec(memory_space=pltpu.SMEM)]
        + [in_vmem]
        + [in_place] * 4,
        out_specs=(in_vmem,) * 3,
        scratch_shapes=[
            pltpu.VMEM((width, 4 * feat_width), bf16),
            pltpu.VMEM((width, feat_width), bf16),
            pltpu.VMEM((width, 2 * hidden), bf16),
            pltpu.VMEM((width, hidden), bf16),
            pltpu.VMEM((row_total, width), bf16),
            pltpu.VMEM((row_total, width), bf16),
            pltpu.VMEM((window + row_total, wide), bf16),
            pltpu.VMEM((window + row_total, wide), bf16),
            pltpu.VMEM((row_total, feat_width), bf16),
            pltpu.VMEM((peers, own_rows, width), bf16),
            pltpu.VMEM((row_total, hidden), bf16),
            pltpu.VMEM((2 * ring_size, row_total, half), bf16),
            pltpu.VMEM((peers, 2 * ring_size, own_rows, half), bf16),
            ring_sems,
            ring_sems,
            pltpu.SemaphoreType.DMA((4,)),
            peer_sems,
            peer_sems,
            peer_sems,
            peer_sems,
            peer_sems,
            peer_sems,
            down_sems,
            down_sems,
        ],
        compiler_params=pltpu.CompilerParams(
            collective_id=0, has_side_effects=True, vmem_limit_bytes=63 * 1024 * 1024
        ),
    )(
        tokens,
        norm_gain.reshape(1, width),
        ffn_gain.reshape(1, width),
        widen(conv_taps),
        past_cache[0],
        cached_len,
        spread,
        mix_weight.reshape(shard_rows, 4 * feat_width),
        out_weight.T,
        ffn_weight.reshape(shard_rows, 2 * hidden),
        down_weight.T,
    )
    ffn_part = jnp.transpose(ffn_sum, (1, 0, 2)).reshape(own_rows, width)
    layer_out = (residual.astype(f32) + ffn_part).astype(bf16)
    return (layer_out, renewed[None])


def solution(mesh):
    in_specs = (
        P(("req", "tp"), None),
        P(),
        P(),
        P("req", None, "tp"),
        P("tp", "req"),
        P("req", None, "tp"),
        P("tp", "req"),
        P(None, "tp"),
        P("req", None, None, "tp"),
        P("req"),
    )
    out_specs = (P(("req", "tp"), None), P("req", None, None, "tp"))
    ring_size, group_size = mesh.shape["req"], mesh.shape["tp"]

    def device_layer(*args):
        tokens, mix_weight, ffn_weight = args[0], args[3], args[5]
        shard_rows, _, feat_width = mix_weight.shape
        fits = (
            ring_size == 8
            and group_size == 4
            and shard_rows % 32 == 0
            and feat_width % (HD * 4) == 0
            and feat_width * 4 == ffn_weight.shape[2]
            and tokens.shape[1] == 8 * shard_rows
            and ffn_weight.shape[2] >= 1024
            and ffn_weight.shape[2] % 256 == 0
            and tokens.shape[0] == 256
        )
        if fits:
            return fused(ring_size, group_size, *args)
        return local(*args)

    return jax.shard_map(
        device_layer, mesh=mesh, in_specs=in_specs, out_specs=out_specs, check_vma=False
    )
```

```python
import functools
import math

import jax
import jax.numpy as jnp
import numpy as np
from jax import lax
from jax.experimental import pallas as pl
from jax.experimental.pallas import tpu as pltpu
from jax.sharding import PartitionSpec as P

HD = 112
WIN = 64


def normed(row_vals, gain):
    floats = row_vals.astype(jnp.float32)
    scaled = floats * lax.rsqrt(jnp.mean(floats * floats, axis=-1, keepdims=True) + 1e-05)
    return (scaled * gain).astype(jnp.bfloat16)


def window_attend(queries, key_rows, value_rows, length, window):
    row_count, head_count, head_size = queries.shape
    block_rows = min(512, row_count)
    score_scale = 1.0 / math.sqrt(head_size)

    def one_block(block_index):
        begin_row = block_index * block_rows
        query_block = lax.dynamic_slice_in_dim(queries, begin_row, block_rows, 0)
        key_block = lax.dynamic_slice_in_dim(key_rows, begin_row, block_rows + window, 0)
        value_block = lax.dynamic_slice_in_dim(value_rows, begin_row, block_rows + window, 0)
        scores = (
            jnp.einsum("qhd,khd->hqk", query_block, key_block, preferred_element_type=jnp.float32)
            * score_scale
        )
        row_ids = begin_row + jnp.arange(block_rows, dtype=jnp.int32)[:, None]
        col_ids = begin_row + jnp.arange(block_rows + window, dtype=jnp.int32)[None, :]
        usable = (col_ids > row_ids) & (col_ids <= row_ids + window) & (col_ids >= window - length)
        scores = jnp.where(usable[None], scores, -1e30)
        row_max = jnp.max(scores, axis=-1, keepdims=True)
        exponent = jnp.exp(scores - row_max)
        weights = (exponent / jnp.sum(exponent, axis=-1, keepdims=True)).astype(jnp.bfloat16)
        return jnp.einsum("hqk,khd->qhd", weights, value_block, preferred_element_type=jnp.float32)

    blocks = lax.map(one_block, jnp.arange(row_count // block_rows, dtype=jnp.int32))
    return blocks.reshape(row_count, head_count, head_size)


def mix_request(projected, cache_rows, length, tap_table, window, head_size):
    row_count, feat_width = (projected.shape[0], projected.shape[2])
    time_order = (length + jnp.arange(window, dtype=jnp.int32)) % window
    earlier = cache_rows[:, time_order]
    key_rows = jnp.concatenate([earlier[0], projected[:, 1]], axis=0)
    value_rows = jnp.concatenate([earlier[1], projected[:, 2]], axis=0)
    head_count = feat_width // head_size
    attended = window_attend(
        projected[:, 0].reshape(row_count, head_count, head_size),
        key_rows.reshape(-1, head_count, head_size),
        value_rows.reshape(-1, head_count, head_size),
        length,
        window,
    ).reshape(row_count, feat_width)
    positions = jnp.arange(window + row_count, dtype=jnp.int32)
    alive_mask = (positions >= window - length)[:, None]
    masked_values = jnp.where(alive_mask, value_rows.astype(jnp.float32), jnp.float32(0.0))
    tap_count = tap_table.shape[0]
    convolved = jnp.zeros((row_count, feat_width), jnp.float32)
    for tap_index in range(tap_count):
        begin_row = window - (tap_count - 1) + tap_index
        convolved = (
            convolved + tap_table[tap_index] * masked_values[begin_row : begin_row + row_count]
        )
    mixed_heads = (attended + projected[:, 3].astype(jnp.float32) * convolved).astype(jnp.bfloat16)
    slot_source = (
        row_count - window + (jnp.arange(window, dtype=jnp.int32) - length - row_count) % window
    )
    renewed = jnp.stack([projected[:, 1], projected[:, 2]])[:, slot_source]
    return (mixed_heads, renewed)


def add_rows(left, shard_piece):
    return jnp.dot(
        left, shard_piece.reshape(shard_piece.shape[0], -1), preferred_element_type=jnp.float32
    )


def local(
    tokens,
    norm_gain,
    ffn_gain,
    mix_weight,
    out_weight,
    ffn_weight,
    down_weight,
    conv_taps,
    past_cache,
    cached_len,
):
    feat_width = mix_weight.shape[2]
    ffn_width = ffn_weight.shape[2]
    normed_all = lax.all_gather(normed(tokens, norm_gain), "tp", axis=0, tiled=True)
    row_total = normed_all.shape[0]
    projected = add_rows(normed_all, lax.all_gather(mix_weight, "req", axis=0, tiled=True))
    projected = projected.astype(jnp.bfloat16).reshape(row_total, 4, feat_width)
    mixed_heads, renewed = mix_request(projected, past_cache[0], cached_len[0], conv_taps, WIN, HD)
    out_columns = lax.all_gather(out_weight, "req", axis=1, tiled=True)
    attn_part = lax.psum_scatter(
        jnp.dot(mixed_heads, out_columns, preferred_element_type=jnp.float32).astype(jnp.bfloat16),
        "tp",
        scatter_dimension=0,
        tiled=True,
    ).astype(jnp.float32)
    residual = (tokens.astype(jnp.float32) + attn_part).astype(jnp.bfloat16)
    ffn_in = lax.all_gather(normed(residual, ffn_gain), "tp", axis=0, tiled=True)
    gate_up = add_rows(ffn_in, lax.all_gather(ffn_weight, "req", axis=0, tiled=True))
    down_columns = lax.all_gather(down_weight, "req", axis=1, tiled=True)
    activated = (jax.nn.silu(gate_up[:, :ffn_width]) * gate_up[:, ffn_width:]).astype(jnp.bfloat16)
    ffn_part = lax.psum_scatter(
        jnp.dot(activated, down_columns, preferred_element_type=jnp.float32).astype(jnp.bfloat16),
        "tp",
        scatter_dimension=0,
        tiled=True,
    ).astype(jnp.float32)
    layer_out = (residual.astype(jnp.float32) + ffn_part).astype(jnp.bfloat16)
    return (layer_out, renewed[None])

MESH = pl.DeviceIdType.MESH


def ring_spot(req_index, ring_size):
    z_index, y_index = req_index // 2, req_index % 2
    return z_index * (1 - y_index) + (ring_size - 1 - z_index) * y_index


def spot_req(spot, ring_size):
    side = spot // (ring_size // 2)
    return 2 * (spot * (1 - side) + (ring_size - 1 - spot) * side) + side


def layer_kernel(
    ring_size,
    group_size,
    window,
    head_count,
    head_size,
    tokens_ref,
    norm_gain_ref,
    ffn_gain_ref,
    taps_ref,
    cache_ref,
    length_ref,
    spread_ref,
    mix_ref,
    out_ref,
    ffn_ref,
    down_ref,
    layer_out_ref,
    renewed_ref,
    mix_all,
    out_all,
    ffn_all,
    down_all,
    normed_all,
    ffn_in_all,
    key_rows,
    value_rows,
    mixed,
    attn_got,
    shared,
    down_part,
    down_got,
    ffn_sum,
    residual_own,
    ring_send,
    ring_recv,
    own_sem,
    gather_send,
    gather_recv,
    attn_send,
    attn_recv,
    ffn_send,
    ffn_recv,
    down_send,
    down_recv,
):
    my_req, my_tp = lax.axis_index("req"), lax.axis_index("tp")
    spot = ring_spot(my_req, ring_size)
    right = spot_req((spot + 1) % ring_size, ring_size)
    left = spot_req((spot + ring_size - 1) % ring_size, ring_size)
    own_rows, width = tokens_ref.shape
    row_total = own_rows * group_size
    shard_rows = mix_ref.shape[0]
    half = shard_rows // 2
    feat_width = out_all.shape[1]
    hidden = ffn_all.shape[1] // 2
    half_cols = mix_ref.shape[1] // 2
    wide = head_count * 128
    last = ring_size - 2

    tile_count = hidden // 256
    early_tiles = (tile_count + 1) // 2
    early_hidden = early_tiles * 256

    streams = [
        (out_ref, out_all, 0, feat_width),
        (mix_ref, mix_all, 0, half_cols),
        (mix_ref, mix_all, half_cols, half_cols),
        (ffn_ref, ffn_all, 0, early_hidden),
        (ffn_ref, ffn_all, hidden, early_hidden),
        (ffn_ref, ffn_all, early_hidden, hidden - early_hidden),
        (ffn_ref, ffn_all, hidden + early_hidden, hidden - early_hidden),
        (down_ref, down_all, 0, hidden // 2),
        (down_ref, down_all, hidden // 2, hidden // 2),
    ]
    mix_phase, early_phase, late_phase, down_phase = (
        ((1,), (2, 0)),
        ((3,), (4,)),
        ((5,), (6,)),
        ((7,), (8,)),
    )

    def shard_req(direction, step):
        if direction == 0:
            return spot_req((spot + ring_size - step) % ring_size, ring_size)
        return spot_req((spot + step) % ring_size, ring_size)

    def half_begin(direction, step):
        return pl.multiple_of(shard_req(direction, step) * shard_rows + direction * half, 16)

    def ring_copy(stream, direction, step, first):
        source, whole, col_begin, col_count = streams[stream]
        cols = pl.ds(col_begin, col_count)
        place = whole.at[pl.ds(half_begin(direction, step), half), cols]
        sem_index = (stream * 2 + direction) * (ring_size - 1) + step
        return pltpu.make_async_remote_copy(
            src_ref=source.at[pl.ds(direction * half, half), cols] if first else place,
            dst_ref=place,
            send_sem=ring_send.at[sem_index],
            recv_sem=ring_recv.at[sem_index],
            device_id={"req": left if direction else right},
            device_id_type=MESH,
        )

    def ring_arrived(stream, direction, step):
        _, whole, col_begin, col_count = streams[stream]
        place = whole.at[
            pl.ds(half_begin(direction, step + 1), half), pl.ds(col_begin, col_count)
        ]
        sem_index = (stream * 2 + direction) * (ring_size - 1) + step
        pltpu.make_async_remote_copy(
            src_ref=place,
            dst_ref=place,
            send_sem=ring_send.at[sem_index],
            recv_sem=ring_recv.at[sem_index],
            device_id={"req": left if direction else right},
            device_id_type=MESH,
        ).wait_recv()

    def begin(lane):
        for stream in lane:
            for direction in range(2):
                ring_copy(stream, direction, 0, True).start()

    def tick(lane, step):
        for stream in lane:
            for direction in range(2):
                ring_arrived(stream, direction, step - 1)
                ring_copy(stream, direction, step, False).start()

    def ticks(phase, low, high):
        @pl.loop(low, high)
        def _(step):
            for lane in phase:
                tick(lane, step)

    def turn(phase, following):
        for lane, next_lane in zip(phase, following):
            tick(lane, last)
            begin(next_lane)

    def finish(phase):
        for lane in phase:
            for stream in lane:
                for direction in range(2):
                    ring_arrived(stream, direction, last)

    def own_copy(index):
        source, whole = ((mix_ref, mix_all), (out_ref, out_all), (ffn_ref, ffn_all), (down_ref, down_all))[index]
        begin_row = pl.multiple_of(my_req * shard_rows, 16)
        return pltpu.make_async_copy(
            source, whole.at[pl.ds(begin_row, shard_rows)], own_sem.at[index]
        )

    def peer(distance):
        return (my_tp + distance) % group_size

    def group_rows(member):
        return pl.ds(pl.multiple_of(member * own_rows, 16), own_rows)

    sibling = my_tp + 1 - 2 * (my_tp % 2)
    across = peer(2)
    diagonal = (sibling + 2) % group_size

    def peer_copy(source, target, sends, recvs, index, member):
        return pltpu.make_async_remote_copy(
            src_ref=source,
            dst_ref=target,
            send_sem=sends.at[index],
            recv_sem=recvs.at[index],
            device_id={"tp": member},
            device_id_type=MESH,
        )

    def gather_copy(whole, sends, recvs, index):
        rows = whole.at[group_rows(across if index == 2 else my_tp)]
        return peer_copy(rows, rows, sends, recvs, index, sibling if index else across)

    def gather_arrived(whole, sends, recvs, index):
        rows = whole.at[group_rows((across, sibling, diagonal)[index])]
        peer_copy(rows, rows, sends, recvs, index, sibling if index else across).wait_recv()

    def attn_copy(index):
        rows = normed_all.at[group_rows((sibling, diagonal, across)[index])]
        return peer_copy(
            rows, attn_got.at[index], attn_send, attn_recv, index, across if index == 2 else sibling
        )

    def down_copy(distance, direction, step):
        block = shard_req(direction, step) * 2 + direction
        sem_index = ((distance - 1) * 2 + direction) * ring_size + step
        return pltpu.make_async_remote_copy(
            src_ref=down_part.at[block, group_rows(peer(distance))],
            dst_ref=down_got.at[distance - 1, block],
            send_sem=down_send.at[sem_index],
            recv_sem=down_recv.at[sem_index],
            device_id={"tp": peer(distance)},
            device_id_type=MESH,
        )

    def rows_dot(a, b):
        return lax.dot_general(
            a, b, (((1,), (1,)), ((), ())), preferred_element_type=jnp.float32
        )

    barrier = pltpu.get_barrier_semaphore()
    for neighbour in (left, right):
        pl.semaphore_signal(
            barrier, inc=1, device_id={"req": neighbour}, device_id_type=MESH
        )
    for distance in range(1, group_size):
        pl.semaphore_signal(
            barrier, inc=1, device_id={"tp": peer(distance)}, device_id_type=MESH
        )
    pl.semaphore_wait(barrier, 1 + group_size)

    begin(mix_phase[0])
    normed_all[group_rows(my_tp), :] = normed(tokens_ref[...], norm_gain_ref[...])
    begin(mix_phase[1])
    for index in range(4):
        own_copy(index).start()
    for index in range(2):
        gather_copy(normed_all, gather_send, gather_recv, index).start()

    length = length_ref[0]
    row_ids = lax.broadcasted_iota(jnp.int32, (window, window), 0)
    col_ids = lax.broadcasted_iota(jnp.int32, (window, window), 1)
    slot_order = ((col_ids - row_ids - length) & (window - 1)) == 0
    slot_order = jnp.where(slot_order, 1.0, 0.0).astype(jnp.bfloat16)
    slot_back = ((row_ids - col_ids - length - row_total) & (window - 1)) == 0
    slot_back = jnp.where(slot_back, 1.0, 0.0).astype(jnp.bfloat16)
    spread_one = spread_ref[0:feat_width, 0:wide]
    for part, rows_ref in ((0, key_rows), (1, value_rows)):
        earlier = jnp.dot(slot_order, cache_ref[part], preferred_element_type=jnp.float32)
        rows_ref[0:window, :] = jnp.dot(
            earlier.astype(jnp.bfloat16), spread_one, preferred_element_type=jnp.float32
        ).astype(jnp.bfloat16)

    ticks(mix_phase, 1, 4)
    gather_arrived(normed_all, gather_send, gather_recv, 0)
    gather_copy(normed_all, gather_send, gather_recv, 2).start()
    ticks(mix_phase, 4, last)
    turn(mix_phase, early_phase)
    for index in (1, 2):
        gather_arrived(normed_all, gather_send, gather_recv, index)
    own_copy(0).wait()
    own_copy(1).wait()
    finish(mix_phase)

    @pl.loop(0, mix_all.shape[1] // 256)
    def _(tile):
        cols = pl.ds(pl.multiple_of(tile * 256, 256), 256)
        shared[:, cols] = jnp.dot(
            normed_all[...], mix_all[:, cols], preferred_element_type=jnp.float32
        ).astype(jnp.bfloat16)

        @pl.when(tile == 3)
        def _():
            tick(early_phase[0], 1)

    block_rows = 128
    key_count = block_rows + window
    score_scale = 1.0 / math.sqrt(head_size)

    def attend(block):
        begin_row = pl.multiple_of(block * block_rows, 128)
        rows = pl.ds(begin_row, block_rows)
        left_half = jnp.dot(
            shared[rows, 0 : 2 * feat_width], spread_ref[...], preferred_element_type=jnp.float32
        ).astype(jnp.bfloat16)
        right_half = jnp.dot(
            shared[rows, 2 * feat_width : 4 * feat_width],
            spread_ref[...],
            preferred_element_type=jnp.float32,
        )
        new_rows = pl.ds(pl.multiple_of(block * block_rows + window, 64), block_rows)
        key_rows[new_rows, :] = left_half[:, wide:]
        value_rows[new_rows, :] = right_half[:, :wide].astype(jnp.bfloat16)
        keys = key_rows[pl.ds(begin_row, key_count), :]
        values = value_rows[pl.ds(begin_row, key_count), :]
        query_ids = lax.broadcasted_iota(jnp.int32, (block_rows, key_count), 0)
        key_ids = lax.broadcasted_iota(jnp.int32, (block_rows, key_count), 1)
        usable = (
            (key_ids > query_ids)
            & (key_ids <= query_ids + window)
            & (key_ids + begin_row >= window - length)
        )
        attended = []
        for head in range(head_count):
            cols = slice(head * 128, head * 128 + 128)
            scores = rows_dot(left_half[:, cols], keys[:, cols]) * score_scale
            scores = jnp.where(usable, scores, -1e30)
            exponent = jnp.exp(scores - jnp.max(scores, axis=-1, keepdims=True))
            weights = exponent / jnp.sum(exponent, axis=-1, keepdims=True)
            attended.append(
                jnp.dot(
                    weights.astype(jnp.bfloat16),
                    values[:, cols],
                    preferred_element_type=jnp.float32,
                )
            )
        attended = jnp.concatenate(attended, axis=1)
        live_ids = lax.broadcasted_iota(jnp.int32, (key_count, wide), 0) + begin_row
        live = jnp.where(live_ids >= window - length, values.astype(jnp.float32), 0.0)
        tap_count = taps_ref.shape[0]
        convolved = jnp.zeros((block_rows, wide), jnp.float32)
        for tap in range(tap_count):
            shift = tap_count - 1 - tap
            moved = pltpu.roll(live, shift, 0) if shift else live
            convolved = convolved + taps_ref[tap : tap + 1, :] * moved[window:, :]
        gates = right_half[:, wide:]
        heads = (attended + gates * convolved).astype(jnp.bfloat16)
        mixed[rows, :] = rows_dot(heads, spread_one).astype(jnp.bfloat16)

    block_total = row_total // block_rows
    tick(early_phase[1], 1)

    @pl.loop(0, block_total)
    def _(block):
        attend(block)

        for side in range(2):

            @pl.when(block % 3 == 1 + side)
            def _():
                tick(early_phase[side], 2 + block // 3)

    for part, rows_ref in ((0, key_rows), (1, value_rows)):
        tail = jnp.dot(
            slot_back,
            rows_ref[row_total : row_total + window, :],
            preferred_element_type=jnp.float32,
        )
        renewed_ref[part] = rows_dot(tail.astype(jnp.bfloat16), spread_one).astype(jnp.bfloat16)

    for index in range(3):
        gather_copy(normed_all, gather_send, gather_recv, index).wait_send()
    tick(early_phase[1], 4)
    for index, member in enumerate((sibling, diagonal, across, my_tp)):
        rows = group_rows(member)
        normed_all[rows, :] = rows_dot(mixed[rows, :], out_all[...]).astype(jnp.bfloat16)
        if index < 2:
            attn_copy(index).start()
        if index == 1:
            tick(early_phase[0], 5)
    tick(early_phase[1], 5)
    attn_copy(1).wait_recv()
    rows = group_rows(across)
    normed_all[rows, :] = (
        normed_all[rows, :].astype(jnp.float32) + attn_got[1].astype(jnp.float32)
    ).astype(jnp.bfloat16)
    attn_copy(2).start()
    turn(early_phase, late_phase)
    own_copy(2).wait()
    own_copy(3).wait()
    finish(early_phase)
    attn_sum = normed_all[group_rows(my_tp), :].astype(jnp.float32)
    for index in (0, 2):
        attn_copy(index).wait_recv()
        attn_sum = attn_sum + attn_got[index].astype(jnp.float32)
    residual = (tokens_ref[...].astype(jnp.float32) + attn_sum).astype(jnp.bfloat16)
    residual_own[...] = residual
    ffn_in_all[group_rows(my_tp), :] = normed(residual, ffn_gain_ref[...])
    for index in range(2):
        gather_copy(ffn_in_all, ffn_send, ffn_recv, index).start()

    ticks(late_phase, 1, 4)
    gather_arrived(ffn_in_all, ffn_send, ffn_recv, 0)
    gather_copy(ffn_in_all, ffn_send, ffn_recv, 2).start()
    for index in (1, 2):
        gather_arrived(ffn_in_all, ffn_send, ffn_recv, index)

    def activate(tile):
        begin_col = pl.multiple_of(tile * 256, 256)
        gate = jnp.dot(
            ffn_in_all[...], ffn_all[:, pl.ds(begin_col, 256)], preferred_element_type=jnp.float32
        )
        up = jnp.dot(
            ffn_in_all[...],
            ffn_all[:, pl.ds(pl.multiple_of(hidden + begin_col, 256), 256)],
            preferred_element_type=jnp.float32,
        )
        activated = gate / (1.0 + jnp.exp(-gate)) * up
        shared[:, pl.ds(begin_col, 256)] = activated.astype(jnp.bfloat16)

    @pl.loop(0, early_tiles)
    def _(tile):
        activate(tile)

        for side in range(2):

            @pl.when(tile % 2 == side)
            def _():
                tick(late_phase[side], 4 + tile // 2)

    turn(late_phase, down_phase)
    finish(late_phase)

    @pl.loop(early_tiles, tile_count)
    def _(tile):
        activate(tile)

        @pl.when(tile == early_tiles)
        def _():
            tick(down_phase[0], 1)

        @pl.when(tile == early_tiles + 1)
        def _():
            tick(down_phase[1], 1)

    def consume(step, directions=(0, 1)):
        for direction in directions:
            block = shard_req(direction, step) * 2 + direction
            down_part[block] = rows_dot(
                shared[...], down_all[pl.ds(half_begin(direction, step), half), :]
            ).astype(jnp.bfloat16)
            for distance in range(1, group_size):
                down_copy(distance, direction, step).start()

    tick(down_phase[0], 2)
    consume(0)
    tick(down_phase[1], 2)
    consume(1)

    @pl.loop(3, last + 1)
    def _(step):
        for side in range(2):
            tick(down_phase[side], step)
            consume(step - 1, (side,))

    consume(last)
    finish(down_phase)
    consume(ring_size - 1)

    @pl.loop(0, ring_size)
    def _(step):
        for direction in range(2):
            block = shard_req(direction, step) * 2 + direction
            total = down_part[block, group_rows(my_tp), :].astype(jnp.float32)
            for distance in range(1, group_size):
                down_copy(distance, direction, step).wait_recv()
                total = total + down_got[distance - 1, block].astype(jnp.float32)
            ffn_sum[block] = total

    for part in range(2):
        rows = slice(part * (own_rows // 2), (part + 1) * (own_rows // 2))
        ffn_part = jnp.concatenate(
            [ffn_sum[block, rows, :] for block in range(2 * ring_size)], axis=1
        )
        layer_out_ref[rows, :] = (
            residual_own[rows, :].astype(jnp.float32) + ffn_part
        ).astype(jnp.bfloat16)

    for stream in range(len(streams)):
        for direction in range(2):
            ring_copy(stream, direction, 0, True).wait_send()

            @pl.loop(1, last + 1)
            def _(step):
                ring_copy(stream, direction, step, False).wait_send()

    for index in range(3):
        attn_copy(index).wait_send()
        gather_copy(ffn_in_all, ffn_send, ffn_recv, index).wait_send()
    for distance in range(1, group_size):

        @pl.loop(0, ring_size)
        def _(step):
            for direction in range(2):
                down_copy(distance, direction, step).wait_send()


def fused(
    ring_size,
    group_size,
    tokens,
    norm_gain,
    ffn_gain,
    mix_weight,
    out_weight,
    ffn_weight,
    down_weight,
    conv_taps,
    past_cache,
    cached_len,
):
    own_rows, width = tokens.shape
    row_total = own_rows * group_size
    shard_rows, _, feat_width = mix_weight.shape
    hidden = ffn_weight.shape[2]
    half = shard_rows // 2
    head_count = feat_width // HD
    wide = head_count * 128
    window = past_cache.shape[2]

    def widen(array):
        heads = array.reshape(array.shape[0], head_count, HD)
        return jnp.pad(heads, ((0, 0), (0, 0), (0, 128 - HD))).reshape(array.shape[0], wide)

    spread_table = np.zeros((2, feat_width, 2, head_count, 128), np.float32)
    for part in range(2):
        for feature in range(feat_width):
            spread_table[part, feature, part, feature // HD, feature % HD] = 1.0
    spread = jnp.asarray(spread_table.reshape(2 * feat_width, 2 * wide), jnp.bfloat16)
    bf16, f32 = jnp.bfloat16, jnp.float32
    in_vmem = pl.BlockSpec(memory_space=pltpu.VMEM)
    in_place = pl.BlockSpec(memory_space=pl.ANY)
    peers = group_size - 1
    ring_sems = pltpu.SemaphoreType.DMA((9 * 2 * (ring_size - 1),))
    peer_sems = pltpu.SemaphoreType.DMA((peers,))
    down_sems = pltpu.SemaphoreType.DMA((peers * 2 * ring_size,))
    layer_out, renewed = pl.pallas_call(
        functools.partial(layer_kernel, ring_size, group_size, window, head_count, HD),
        out_shape=(
            jax.ShapeDtypeStruct((own_rows, width), bf16),
            jax.ShapeDtypeStruct((2, window, feat_width), bf16),
        ),
        in_specs=[in_vmem] * 5
        + [pl.BlockSpec(memory_space=pltpu.SMEM)]
        + [in_vmem]
        + [in_place] * 4,
        out_specs=(in_vmem,) * 2,
        scratch_shapes=[
            pltpu.VMEM((width, 4 * feat_width), bf16),
            pltpu.VMEM((width, feat_width), bf16),
            pltpu.VMEM((width, 2 * hidden), bf16),
            pltpu.VMEM((width, hidden), bf16),
            pltpu.VMEM((row_total, width), bf16),
            pltpu.VMEM((row_total, width), bf16),
            pltpu.VMEM((window + row_total, wide), bf16),
            pltpu.VMEM((window + row_total, wide), bf16),
            pltpu.VMEM((row_total, feat_width), bf16),
            pltpu.VMEM((peers, own_rows, width), bf16),
            pltpu.VMEM((row_total, hidden), bf16),
            pltpu.VMEM((2 * ring_size, row_total, half), bf16),
            pltpu.VMEM((peers, 2 * ring_size, own_rows, half), bf16),
            pltpu.VMEM((2 * ring_size, own_rows, half), f32),
            pltpu.VMEM((own_rows, width), bf16),
            ring_sems,
            ring_sems,
            pltpu.SemaphoreType.DMA((4,)),
            peer_sems,
            peer_sems,
            peer_sems,
            peer_sems,
            peer_sems,
            peer_sems,
            down_sems,
            down_sems,
        ],
        compiler_params=pltpu.CompilerParams(
            collective_id=0, has_side_effects=True, vmem_limit_bytes=63 * 1024 * 1024
        ),
    )(
        tokens,
        norm_gain.reshape(1, width),
        ffn_gain.reshape(1, width),
        widen(conv_taps),
        past_cache[0],
        cached_len,
        spread,
        mix_weight.reshape(shard_rows, 4 * feat_width),
        out_weight.T,
        ffn_weight.reshape(shard_rows, 2 * hidden),
        down_weight.T,
    )
    return (layer_out, renewed[None])


def solution(mesh):
    in_specs = (
        P(("req", "tp"), None),
        P(),
        P(),
        P("req", None, "tp"),
        P("tp", "req"),
        P("req", None, "tp"),
        P("tp", "req"),
        P(None, "tp"),
        P("req", None, None, "tp"),
        P("req"),
    )
    out_specs = (P(("req", "tp"), None), P("req", None, None, "tp"))
    ring_size, group_size = mesh.shape["req"], mesh.shape["tp"]

    def device_layer(*args):
        tokens, mix_weight, ffn_weight = args[0], args[3], args[5]
        shard_rows, _, feat_width = mix_weight.shape
        fits = (
            ring_size == 8
            and group_size == 4
            and shard_rows % 32 == 0
            and feat_width % (HD * 4) == 0
            and feat_width * 4 == ffn_weight.shape[2]
            and tokens.shape[1] == 8 * shard_rows
            and ffn_weight.shape[2] == 7 * 256
            and tokens.shape[0] == 256
        )
        if fits:
            return fused(ring_size, group_size, *args)
        return local(*args)

    return jax.shard_map(
        device_layer, mesh=mesh, in_specs=in_specs, out_specs=out_specs, check_vma=False
    )
```

```python
import functools
import math

import jax
import jax.numpy as jnp
import numpy as np
from jax import lax
from jax.experimental import pallas as pl
from jax.experimental.pallas import tpu as pltpu
from jax.sharding import PartitionSpec as P

HD = 112
WIN = 64


def normed(row_vals, gain):
    floats = row_vals.astype(jnp.float32)
    scaled = floats * lax.rsqrt(jnp.mean(floats * floats, axis=-1, keepdims=True) + 1e-05)
    return (scaled * gain).astype(jnp.bfloat16)


def window_attend(queries, key_rows, value_rows, length, window):
    row_count, head_count, head_size = queries.shape
    block_rows = min(512, row_count)
    score_scale = 1.0 / math.sqrt(head_size)

    def one_block(block_index):
        begin_row = block_index * block_rows
        query_block = lax.dynamic_slice_in_dim(queries, begin_row, block_rows, 0)
        key_block = lax.dynamic_slice_in_dim(key_rows, begin_row, block_rows + window, 0)
        value_block = lax.dynamic_slice_in_dim(value_rows, begin_row, block_rows + window, 0)
        scores = (
            jnp.einsum("qhd,khd->hqk", query_block, key_block, preferred_element_type=jnp.float32)
            * score_scale
        )
        row_ids = begin_row + jnp.arange(block_rows, dtype=jnp.int32)[:, None]
        col_ids = begin_row + jnp.arange(block_rows + window, dtype=jnp.int32)[None, :]
        usable = (col_ids > row_ids) & (col_ids <= row_ids + window) & (col_ids >= window - length)
        scores = jnp.where(usable[None], scores, -1e30)
        row_max = jnp.max(scores, axis=-1, keepdims=True)
        exponent = jnp.exp(scores - row_max)
        weights = (exponent / jnp.sum(exponent, axis=-1, keepdims=True)).astype(jnp.bfloat16)
        return jnp.einsum("hqk,khd->qhd", weights, value_block, preferred_element_type=jnp.float32)

    blocks = lax.map(one_block, jnp.arange(row_count // block_rows, dtype=jnp.int32))
    return blocks.reshape(row_count, head_count, head_size)


def mix_request(projected, cache_rows, length, tap_table, window, head_size):
    row_count, feat_width = (projected.shape[0], projected.shape[2])
    time_order = (length + jnp.arange(window, dtype=jnp.int32)) % window
    earlier = cache_rows[:, time_order]
    key_rows = jnp.concatenate([earlier[0], projected[:, 1]], axis=0)
    value_rows = jnp.concatenate([earlier[1], projected[:, 2]], axis=0)
    head_count = feat_width // head_size
    attended = window_attend(
        projected[:, 0].reshape(row_count, head_count, head_size),
        key_rows.reshape(-1, head_count, head_size),
        value_rows.reshape(-1, head_count, head_size),
        length,
        window,
    ).reshape(row_count, feat_width)
    positions = jnp.arange(window + row_count, dtype=jnp.int32)
    alive_mask = (positions >= window - length)[:, None]
    masked_values = jnp.where(alive_mask, value_rows.astype(jnp.float32), jnp.float32(0.0))
    tap_count = tap_table.shape[0]
    convolved = jnp.zeros((row_count, feat_width), jnp.float32)
    for tap_index in range(tap_count):
        begin_row = window - (tap_count - 1) + tap_index
        convolved = (
            convolved + tap_table[tap_index] * masked_values[begin_row : begin_row + row_count]
        )
    mixed_heads = (attended + projected[:, 3].astype(jnp.float32) * convolved).astype(jnp.bfloat16)
    slot_source = (
        row_count - window + (jnp.arange(window, dtype=jnp.int32) - length - row_count) % window
    )
    renewed = jnp.stack([projected[:, 1], projected[:, 2]])[:, slot_source]
    return (mixed_heads, renewed)


def add_rows(left, shard_piece):
    return jnp.dot(
        left, shard_piece.reshape(shard_piece.shape[0], -1), preferred_element_type=jnp.float32
    )


def local(
    tokens,
    norm_gain,
    ffn_gain,
    mix_weight,
    out_weight,
    ffn_weight,
    down_weight,
    conv_taps,
    past_cache,
    cached_len,
):
    feat_width = mix_weight.shape[2]
    ffn_width = ffn_weight.shape[2]
    normed_all = lax.all_gather(normed(tokens, norm_gain), "tp", axis=0, tiled=True)
    row_total = normed_all.shape[0]
    projected = add_rows(normed_all, lax.all_gather(mix_weight, "req", axis=0, tiled=True))
    projected = projected.astype(jnp.bfloat16).reshape(row_total, 4, feat_width)
    mixed_heads, renewed = mix_request(projected, past_cache[0], cached_len[0], conv_taps, WIN, HD)
    out_columns = lax.all_gather(out_weight, "req", axis=1, tiled=True)
    attn_part = lax.psum_scatter(
        jnp.dot(mixed_heads, out_columns, preferred_element_type=jnp.float32).astype(jnp.bfloat16),
        "tp",
        scatter_dimension=0,
        tiled=True,
    ).astype(jnp.float32)
    residual = (tokens.astype(jnp.float32) + attn_part).astype(jnp.bfloat16)
    ffn_in = lax.all_gather(normed(residual, ffn_gain), "tp", axis=0, tiled=True)
    gate_up = add_rows(ffn_in, lax.all_gather(ffn_weight, "req", axis=0, tiled=True))
    down_columns = lax.all_gather(down_weight, "req", axis=1, tiled=True)
    activated = (jax.nn.silu(gate_up[:, :ffn_width]) * gate_up[:, ffn_width:]).astype(jnp.bfloat16)
    ffn_part = lax.psum_scatter(
        jnp.dot(activated, down_columns, preferred_element_type=jnp.float32).astype(jnp.bfloat16),
        "tp",
        scatter_dimension=0,
        tiled=True,
    ).astype(jnp.float32)
    layer_out = (residual.astype(jnp.float32) + ffn_part).astype(jnp.bfloat16)
    return (layer_out, renewed[None])

MESH = pl.DeviceIdType.MESH


def ring_spot(req_index, ring_size):
    z_index, y_index = req_index // 2, req_index % 2
    return z_index * (1 - y_index) + (ring_size - 1 - z_index) * y_index


def spot_req(spot, ring_size):
    side = spot // (ring_size // 2)
    return 2 * (spot * (1 - side) + (ring_size - 1 - spot) * side) + side


def layer_kernel(
    ring_size,
    group_size,
    window,
    head_count,
    head_size,
    tokens_ref,
    norm_gain_ref,
    ffn_gain_ref,
    taps_ref,
    cache_ref,
    length_ref,
    spread_ref,
    mix_ref,
    out_ref,
    ffn_ref,
    down_ref,
    layer_out_ref,
    renewed_ref,
    mix_all,
    out_all,
    ffn_all,
    down_all,
    normed_all,
    ffn_in_all,
    key_rows,
    value_rows,
    mixed,
    attn_got,
    shared,
    down_part,
    down_got,
    ffn_sum,
    residual_own,
    wide_taps,
    ring_send,
    ring_recv,
    own_sem,
    gather_send,
    gather_recv,
    attn_send,
    attn_recv,
    ffn_send,
    ffn_recv,
    down_send,
    down_recv,
):
    my_req, my_tp = lax.axis_index("req"), lax.axis_index("tp")
    spot = ring_spot(my_req, ring_size)
    right = spot_req((spot + 1) % ring_size, ring_size)
    left = spot_req((spot + ring_size - 1) % ring_size, ring_size)
    own_rows, width = tokens_ref.shape
    row_total = own_rows * group_size
    shard_rows = mix_ref.shape[0]
    half = shard_rows // 2
    feat_width = out_all.shape[1]
    hidden = ffn_all.shape[1] // 2
    half_cols = mix_ref.shape[1] // 2
    wide = head_count * 128
    last = ring_size - 2

    tile_count = hidden // 256
    early_tiles = (tile_count + 1) // 2
    early_hidden = early_tiles * 256

    streams = [
        (out_ref, out_all, 0, feat_width),
        (mix_ref, mix_all, 0, half_cols),
        (mix_ref, mix_all, half_cols, half_cols),
        (ffn_ref, ffn_all, 0, early_hidden),
        (ffn_ref, ffn_all, hidden, early_hidden),
        (ffn_ref, ffn_all, early_hidden, hidden - early_hidden),
        (ffn_ref, ffn_all, hidden + early_hidden, hidden - early_hidden),
        (down_ref, down_all, 0, hidden // 2),
        (down_ref, down_all, hidden // 2, hidden // 2),
    ]
    mix_phase, early_phase, late_phase, down_phase = (
        ((1,), (2, 0)),
        ((3,), (4,)),
        ((5,), (6,)),
        ((7,), (8,)),
    )

    def shard_req(direction, step):
        if direction == 0:
            return spot_req((spot + ring_size - step) % ring_size, ring_size)
        return spot_req((spot + step) % ring_size, ring_size)

    def half_begin(direction, step):
        return pl.multiple_of(shard_req(direction, step) * shard_rows + direction * half, 16)

    def ring_copy(stream, direction, step, first):
        source, whole, col_begin, col_count = streams[stream]
        cols = pl.ds(col_begin, col_count)
        place = whole.at[pl.ds(half_begin(direction, step), half), cols]
        sem_index = (stream * 2 + direction) * (ring_size - 1) + step
        return pltpu.make_async_remote_copy(
            src_ref=source.at[pl.ds(direction * half, half), cols] if first else place,
            dst_ref=place,
            send_sem=ring_send.at[sem_index],
            recv_sem=ring_recv.at[sem_index],
            device_id={"req": left if direction else right},
            device_id_type=MESH,
        )

    def ring_arrived(stream, direction, step):
        _, whole, col_begin, col_count = streams[stream]
        place = whole.at[
            pl.ds(half_begin(direction, step + 1), half), pl.ds(col_begin, col_count)
        ]
        sem_index = (stream * 2 + direction) * (ring_size - 1) + step
        pltpu.make_async_remote_copy(
            src_ref=place,
            dst_ref=place,
            send_sem=ring_send.at[sem_index],
            recv_sem=ring_recv.at[sem_index],
            device_id={"req": left if direction else right},
            device_id_type=MESH,
        ).wait_recv()

    def begin(lane):
        for stream in lane:
            for direction in range(2):
                ring_copy(stream, direction, 0, True).start()

    def tick(lane, step):
        for stream in lane:
            for direction in range(2):
                ring_arrived(stream, direction, step - 1)
                ring_copy(stream, direction, step, False).start()

    def ticks(phase, low, high):
        @pl.loop(low, high)
        def _(step):
            for lane in phase:
                tick(lane, step)

    def turn(phase, following):
        for lane, next_lane in zip(phase, following):
            tick(lane, last)
            begin(next_lane)

    def finish(phase):
        for lane in phase:
            for stream in lane:
                for direction in range(2):
                    ring_arrived(stream, direction, last)

    def own_copy(index):
        source, whole = ((mix_ref, mix_all), (out_ref, out_all), (ffn_ref, ffn_all), (down_ref, down_all))[index]
        begin_row = pl.multiple_of(my_req * shard_rows, 16)
        return pltpu.make_async_copy(
            source, whole.at[pl.ds(begin_row, shard_rows)], own_sem.at[index]
        )

    def peer(distance):
        return (my_tp + distance) % group_size

    def group_rows(member):
        return pl.ds(pl.multiple_of(member * own_rows, 16), own_rows)

    sibling = my_tp + 1 - 2 * (my_tp % 2)
    across = peer(2)
    diagonal = (sibling + 2) % group_size

    def peer_copy(source, target, sends, recvs, index, member):
        return pltpu.make_async_remote_copy(
            src_ref=source,
            dst_ref=target,
            send_sem=sends.at[index],
            recv_sem=recvs.at[index],
            device_id={"tp": member},
            device_id_type=MESH,
        )

    def gather_copy(whole, sends, recvs, index):
        rows = whole.at[group_rows(across if index == 2 else my_tp)]
        return peer_copy(rows, rows, sends, recvs, index, sibling if index else across)

    def gather_arrived(whole, sends, recvs, index):
        rows = whole.at[group_rows((across, sibling, diagonal)[index])]
        peer_copy(rows, rows, sends, recvs, index, sibling if index else across).wait_recv()

    def attn_copy(index):
        rows = normed_all.at[group_rows((sibling, diagonal, across)[index])]
        return peer_copy(
            rows, attn_got.at[index], attn_send, attn_recv, index, across if index == 2 else sibling
        )

    def down_copy(distance, direction, step):
        block = shard_req(direction, step) * 2 + direction
        sem_index = ((distance - 1) * 2 + direction) * ring_size + step
        return pltpu.make_async_remote_copy(
            src_ref=down_part.at[block, group_rows(peer(distance))],
            dst_ref=down_got.at[distance - 1, block],
            send_sem=down_send.at[sem_index],
            recv_sem=down_recv.at[sem_index],
            device_id={"tp": peer(distance)},
            device_id_type=MESH,
        )

    def rows_dot(a, b):
        return lax.dot_general(
            a, b, (((1,), (1,)), ((), ())), preferred_element_type=jnp.float32
        )

    barrier = pltpu.get_barrier_semaphore()
    for neighbour in (left, right):
        pl.semaphore_signal(
            barrier, inc=1, device_id={"req": neighbour}, device_id_type=MESH
        )
    for distance in range(1, group_size):
        pl.semaphore_signal(
            barrier, inc=1, device_id={"tp": peer(distance)}, device_id_type=MESH
        )
    pl.semaphore_wait(barrier, 1 + group_size)

    begin(mix_phase[0])
    normed_all[group_rows(my_tp), :] = normed(tokens_ref[...], norm_gain_ref[...].reshape(1, width))
    begin(mix_phase[1])
    for index in range(4):
        own_copy(index).start()
    for index in range(2):
        gather_copy(normed_all, gather_send, gather_recv, index).start()

    length = length_ref[0]
    row_ids = lax.broadcasted_iota(jnp.int32, (window, window), 0)
    col_ids = lax.broadcasted_iota(jnp.int32, (window, window), 1)
    slot_order = ((col_ids - row_ids - length) & (window - 1)) == 0
    slot_order = jnp.where(slot_order, 1.0, 0.0).astype(jnp.bfloat16)
    slot_back = ((row_ids - col_ids - length - row_total) & (window - 1)) == 0
    slot_back = jnp.where(slot_back, 1.0, 0.0).astype(jnp.bfloat16)
    spread_one = spread_ref[0:feat_width, 0:wide]
    taps = jnp.dot(
        taps_ref[...],
        spread_one.astype(jnp.float32),
        precision=lax.Precision.HIGHEST,
        preferred_element_type=jnp.float32,
    )
    wide_taps[...] = taps
    for part, rows_ref in ((0, key_rows), (1, value_rows)):
        earlier = jnp.dot(slot_order, cache_ref[part], preferred_element_type=jnp.float32)
        rows_ref[0:window, :] = jnp.dot(
            earlier.astype(jnp.bfloat16), spread_one, preferred_element_type=jnp.float32
        ).astype(jnp.bfloat16)

    ticks(mix_phase, 1, 4)
    gather_arrived(normed_all, gather_send, gather_recv, 0)
    gather_copy(normed_all, gather_send, gather_recv, 2).start()
    ticks(mix_phase, 4, last)
    turn(mix_phase, early_phase)
    for index in (1, 2):
        gather_arrived(normed_all, gather_send, gather_recv, index)
    own_copy(0).wait()
    own_copy(1).wait()
    finish(mix_phase)

    @pl.loop(0, mix_all.shape[1] // 256)
    def _(tile):
        cols = pl.ds(pl.multiple_of(tile * 256, 256), 256)
        shared[:, cols] = jnp.dot(
            normed_all[...], mix_all[:, cols], preferred_element_type=jnp.float32
        ).astype(jnp.bfloat16)

        @pl.when(tile == 3)
        def _():
            tick(early_phase[0], 1)

    block_rows = 128
    key_count = block_rows + window
    score_scale = 1.0 / math.sqrt(head_size)

    def attend(block):
        begin_row = pl.multiple_of(block * block_rows, 128)
        rows = pl.ds(begin_row, block_rows)
        left_half = jnp.dot(
            shared[rows, 0 : 2 * feat_width], spread_ref[...], preferred_element_type=jnp.float32
        ).astype(jnp.bfloat16)
        right_half = jnp.dot(
            shared[rows, 2 * feat_width : 4 * feat_width],
            spread_ref[...],
            preferred_element_type=jnp.float32,
        )
        new_rows = pl.ds(pl.multiple_of(block * block_rows + window, 64), block_rows)
        key_rows[new_rows, :] = left_half[:, wide:]
        value_rows[new_rows, :] = right_half[:, :wide].astype(jnp.bfloat16)
        keys = key_rows[pl.ds(begin_row, key_count), :]
        values = value_rows[pl.ds(begin_row, key_count), :]
        query_ids = lax.broadcasted_iota(jnp.int32, (block_rows, key_count), 0)
        key_ids = lax.broadcasted_iota(jnp.int32, (block_rows, key_count), 1)
        usable = (
            (key_ids > query_ids)
            & (key_ids <= query_ids + window)
            & (key_ids + begin_row >= window - length)
        )
        attended = []
        for head in range(head_count):
            cols = slice(head * 128, head * 128 + 128)
            scores = rows_dot(left_half[:, cols], keys[:, cols]) * score_scale
            scores = jnp.where(usable, scores, -1e30)
            exponent = jnp.exp(scores - jnp.max(scores, axis=-1, keepdims=True))
            weights = exponent / jnp.sum(exponent, axis=-1, keepdims=True)
            attended.append(
                jnp.dot(
                    weights.astype(jnp.bfloat16),
                    values[:, cols],
                    preferred_element_type=jnp.float32,
                )
            )
        attended = jnp.concatenate(attended, axis=1)
        live_ids = lax.broadcasted_iota(jnp.int32, (key_count, wide), 0) + begin_row
        live = jnp.where(live_ids >= window - length, values.astype(jnp.float32), 0.0)
        tap_count = taps_ref.shape[0]
        convolved = jnp.zeros((block_rows, wide), jnp.float32)
        for tap in range(tap_count):
            shift = tap_count - 1 - tap
            moved = pltpu.roll(live, shift, 0) if shift else live
            convolved = convolved + wide_taps[tap : tap + 1, :] * moved[window:, :]
        gates = right_half[:, wide:]
        heads = (attended + gates * convolved).astype(jnp.bfloat16)
        mixed[rows, :] = rows_dot(heads, spread_one).astype(jnp.bfloat16)

    block_total = row_total // block_rows
    tick(early_phase[1], 1)

    @pl.loop(0, block_total)
    def _(block):
        attend(block)

        for side in range(2):

            @pl.when(block % 3 == 1 + side)
            def _():
                tick(early_phase[side], 2 + block // 3)

    for part, rows_ref in ((0, key_rows), (1, value_rows)):
        tail = jnp.dot(
            slot_back,
            rows_ref[row_total : row_total + window, :],
            preferred_element_type=jnp.float32,
        )
        renewed_ref[part] = rows_dot(tail.astype(jnp.bfloat16), spread_one).astype(jnp.bfloat16)

    for index in range(3):
        gather_copy(normed_all, gather_send, gather_recv, index).wait_send()
    tick(early_phase[1], 4)
    for index, member in enumerate((sibling, diagonal, across, my_tp)):
        rows = group_rows(member)
        normed_all[rows, :] = rows_dot(mixed[rows, :], out_all[...]).astype(jnp.bfloat16)
        if index < 2:
            attn_copy(index).start()
        if index == 1:
            tick(early_phase[0], 5)
    tick(early_phase[1], 5)
    attn_copy(1).wait_recv()
    rows = group_rows(across)
    normed_all[rows, :] = (
        normed_all[rows, :].astype(jnp.float32) + attn_got[1].astype(jnp.float32)
    ).astype(jnp.bfloat16)
    attn_copy(2).start()
    turn(early_phase, late_phase)
    own_copy(2).wait()
    own_copy(3).wait()
    finish(early_phase)
    attn_sum = normed_all[group_rows(my_tp), :].astype(jnp.float32)
    for index in (0, 2):
        attn_copy(index).wait_recv()
        attn_sum = attn_sum + attn_got[index].astype(jnp.float32)
    residual = (tokens_ref[...].astype(jnp.float32) + attn_sum).astype(jnp.bfloat16)
    residual_own[...] = residual
    ffn_in_all[group_rows(my_tp), :] = normed(residual, ffn_gain_ref[...].reshape(1, width))
    for index in range(2):
        gather_copy(ffn_in_all, ffn_send, ffn_recv, index).start()

    ticks(late_phase, 1, 4)
    gather_arrived(ffn_in_all, ffn_send, ffn_recv, 0)
    gather_copy(ffn_in_all, ffn_send, ffn_recv, 2).start()
    for index in (1, 2):
        gather_arrived(ffn_in_all, ffn_send, ffn_recv, index)

    def activate(tile):
        begin_col = pl.multiple_of(tile * 256, 256)
        gate = jnp.dot(
            ffn_in_all[...], ffn_all[:, pl.ds(begin_col, 256)], preferred_element_type=jnp.float32
        )
        up = jnp.dot(
            ffn_in_all[...],
            ffn_all[:, pl.ds(pl.multiple_of(hidden + begin_col, 256), 256)],
            preferred_element_type=jnp.float32,
        )
        activated = gate / (1.0 + jnp.exp(-gate)) * up
        shared[:, pl.ds(begin_col, 256)] = activated.astype(jnp.bfloat16)

    @pl.loop(0, early_tiles)
    def _(tile):
        activate(tile)

        for side in range(2):

            @pl.when(tile % 2 == side)
            def _():
                tick(late_phase[side], 4 + tile // 2)

    turn(late_phase, down_phase)
    finish(late_phase)

    @pl.loop(early_tiles, tile_count)
    def _(tile):
        activate(tile)

        @pl.when(tile == early_tiles)
        def _():
            tick(down_phase[0], 1)

        @pl.when(tile == early_tiles + 1)
        def _():
            tick(down_phase[1], 1)

    def consume(step, directions=(0, 1)):
        for direction in directions:
            block = shard_req(direction, step) * 2 + direction
            down_part[block] = rows_dot(
                shared[...], down_all[pl.ds(half_begin(direction, step), half), :]
            ).astype(jnp.bfloat16)
            for distance in range(1, group_size):
                down_copy(distance, direction, step).start()

    tick(down_phase[0], 2)
    consume(0)
    tick(down_phase[1], 2)
    consume(1)

    @pl.loop(3, last + 1)
    def _(step):
        for side in range(2):
            tick(down_phase[side], step)
            consume(step - 1, (side,))

    consume(last)
    finish(down_phase)
    consume(ring_size - 1)

    @pl.loop(0, ring_size)
    def _(step):
        for direction in range(2):
            block = shard_req(direction, step) * 2 + direction
            total = down_part[block, group_rows(my_tp), :].astype(jnp.float32)
            for distance in range(1, group_size):
                down_copy(distance, direction, step).wait_recv()
                total = total + down_got[distance - 1, block].astype(jnp.float32)
            ffn_sum[block] = total

    for part in range(2):
        rows = slice(part * (own_rows // 2), (part + 1) * (own_rows // 2))
        ffn_part = jnp.concatenate(
            [ffn_sum[block, rows, :] for block in range(2 * ring_size)], axis=1
        )
        layer_out_ref[rows, :] = (
            residual_own[rows, :].astype(jnp.float32) + ffn_part
        ).astype(jnp.bfloat16)

    for stream in range(len(streams)):
        for direction in range(2):
            ring_copy(stream, direction, 0, True).wait_send()

            @pl.loop(1, last + 1)
            def _(step):
                ring_copy(stream, direction, step, False).wait_send()

    for index in range(3):
        attn_copy(index).wait_send()
        gather_copy(ffn_in_all, ffn_send, ffn_recv, index).wait_send()
    for distance in range(1, group_size):

        @pl.loop(0, ring_size)
        def _(step):
            for direction in range(2):
                down_copy(distance, direction, step).wait_send()


def fused(
    ring_size,
    group_size,
    tokens,
    norm_gain,
    ffn_gain,
    mix_weight,
    out_weight,
    ffn_weight,
    down_weight,
    conv_taps,
    past_cache,
    cached_len,
):
    own_rows, width = tokens.shape
    row_total = own_rows * group_size
    shard_rows, _, feat_width = mix_weight.shape
    hidden = ffn_weight.shape[2]
    half = shard_rows // 2
    head_count = feat_width // HD
    wide = head_count * 128
    window = past_cache.shape[2]

    spread_table = np.zeros((2, feat_width, 2, head_count, 128), np.float32)
    for part in range(2):
        for feature in range(feat_width):
            spread_table[part, feature, part, feature // HD, feature % HD] = 1.0
    spread = jnp.asarray(spread_table.reshape(2 * feat_width, 2 * wide), jnp.bfloat16)
    bf16, f32 = jnp.bfloat16, jnp.float32
    in_vmem = pl.BlockSpec(memory_space=pltpu.VMEM)
    in_place = pl.BlockSpec(memory_space=pl.ANY)
    peers = group_size - 1
    ring_sems = pltpu.SemaphoreType.DMA((9 * 2 * (ring_size - 1),))
    peer_sems = pltpu.SemaphoreType.DMA((peers,))
    down_sems = pltpu.SemaphoreType.DMA((peers * 2 * ring_size,))
    layer_out, renewed = pl.pallas_call(
        functools.partial(layer_kernel, ring_size, group_size, window, head_count, HD),
        out_shape=(
            jax.ShapeDtypeStruct((own_rows, width), bf16),
            jax.ShapeDtypeStruct((2, window, feat_width), bf16),
        ),
        in_specs=[in_vmem] * 5
        + [pl.BlockSpec(memory_space=pltpu.SMEM)]
        + [in_vmem]
        + [in_place] * 4,
        out_specs=(in_vmem,) * 2,
        scratch_shapes=[
            pltpu.VMEM((width, 4 * feat_width), bf16),
            pltpu.VMEM((width, feat_width), bf16),
            pltpu.VMEM((width, 2 * hidden), bf16),
            pltpu.VMEM((width, hidden), bf16),
            pltpu.VMEM((row_total, width), bf16),
            pltpu.VMEM((row_total, width), bf16),
            pltpu.VMEM((window + row_total, wide), bf16),
            pltpu.VMEM((window + row_total, wide), bf16),
            pltpu.VMEM((row_total, feat_width), bf16),
            pltpu.VMEM((peers, own_rows, width), bf16),
            pltpu.VMEM((row_total, hidden), bf16),
            pltpu.VMEM((2 * ring_size, row_total, half), bf16),
            pltpu.VMEM((peers, 2 * ring_size, own_rows, half), bf16),
            pltpu.VMEM((2 * ring_size, own_rows, half), f32),
            pltpu.VMEM((own_rows, width), bf16),
            pltpu.VMEM((conv_taps.shape[0], wide), f32),
            ring_sems,
            ring_sems,
            pltpu.SemaphoreType.DMA((4,)),
            peer_sems,
            peer_sems,
            peer_sems,
            peer_sems,
            peer_sems,
            peer_sems,
            down_sems,
            down_sems,
        ],
        compiler_params=pltpu.CompilerParams(
            collective_id=0, has_side_effects=True, vmem_limit_bytes=63 * 1024 * 1024
        ),
    )(
        tokens,
        norm_gain,
        ffn_gain,
        conv_taps,
        past_cache[0],
        cached_len,
        spread,
        mix_weight.reshape(shard_rows, 4 * feat_width),
        out_weight.T,
        ffn_weight.reshape(shard_rows, 2 * hidden),
        down_weight.T,
    )
    return (layer_out, renewed[None])


def solution(mesh):
    in_specs = (
        P(("req", "tp"), None),
        P(),
        P(),
        P("req", None, "tp"),
        P("tp", "req"),
        P("req", None, "tp"),
        P("tp", "req"),
        P(None, "tp"),
        P("req", None, None, "tp"),
        P("req"),
    )
    out_specs = (P(("req", "tp"), None), P("req", None, None, "tp"))
    ring_size, group_size = mesh.shape["req"], mesh.shape["tp"]

    def device_layer(*args):
        tokens, mix_weight, ffn_weight = args[0], args[3], args[5]
        shard_rows, _, feat_width = mix_weight.shape
        fits = (
            ring_size == 8
            and group_size == 4
            and shard_rows % 32 == 0
            and feat_width % (HD * 4) == 0
            and feat_width * 4 == ffn_weight.shape[2]
            and tokens.shape[1] == 8 * shard_rows
            and ffn_weight.shape[2] == 7 * 256
            and tokens.shape[0] == 256
        )
        if fits:
            return fused(ring_size, group_size, *args)
        return local(*args)

    return jax.shard_map(
        device_layer, mesh=mesh, in_specs=in_specs, out_specs=out_specs, check_vma=False
    )
```
